128 devices in a mesh: sub: 32 (over z, x, core), lvl: 4 (over y).
Axes of the slice: x: 4, y: 4, z: 4, core: 2. Of those that a mesh axis runs over, the one named last changes fastest.
Arguments:
- vectors: bfloat16 [4096, 2, 256], P(('sub', 'lvl')), may hold values from -6 to 6
- self_blocks: bfloat16 [4096, 256, 256], P(('sub', 'lvl')), may hold values from -0.375 to 0.375
- near_blocks: bfloat16 [4096, 256, 256], P(('sub', 'lvl')), may hold values from -0.375 to 0.375
- near_row: int32 [4096], P(('sub', 'lvl')), may hold values from 0 to 31
- near_col: int32 [4096], P(('sub', 'lvl')), may hold values from 0 to 63
- bases: bfloat16 [4096, 256, 64], P(('sub', 'lvl')), may hold values from -0.375 to 0.375
- transfers: float32 [7936, 64, 64], P(('sub', 'lvl')), may hold values from -0.5 to 0.5
- far_row: int32 [16384], P(('sub', 'lvl')), may hold values from 0 to 31
- far_col: int32 [16384], P(('sub', 'lvl')), may hold values from 0 to 4095, as said below
- couplings: float32 [16384, 64, 64], P(('sub', 'lvl')), may hold values from -0.75 to 0.75
- root_couplings: float32 [128, 128, 64, 64], P(('sub', 'lvl')), may hold values from -1.5 to 1.5
Outputs:
- products: float32 [4096, 2, 256], P(('sub', 'lvl'))
The draws below stay inside these ranges and needn't reach their ends.
Inputs may be any that keep to these rules, and one draw needn't show every extreme that they name: `far_col`: the column leaf of an admissible pair never lies on the owning device. Of each device's 128 pairs, exactly 16 have column leaves on each of the six devices 1, 2 or 3 places before or after it (cyclically over all devices). The others lie on devices more than 3 places away, at most 16 on any one device, and exactly 16 of them on one such device.
All inputs are finite; a program needn't handle non-finite values.
Results may differ from the reference program's by a relative error of at most 0.0024.
Values may be sent and summed in bfloat16 or wider, within the bound.
A program may use at most 128 MiB of HBM per device.

```python
import jax
import jax.numpy as jnp
from jax import lax

LEAF = 256
RANK = 64
LEAF_DEV = 32
NEAR_DEV = 32
FAR_DEV = 128
LEAVES = 4096
NEAR = 4096
FAR = 16384
TRANS = 7936
N_SUB = 32
N_LVL = 4


def draw_far_col(key, part):
    key = jax.random.fold_in(key, 11)
    devices = N_SUB * N_LVL
    cap = LEAF_DEV // 2
    near_deltas = jnp.repeat(jnp.array([-3, -2, -1, 1, 2, 3], jnp.int32), cap)
    far_count = devices - 7
    spread_count = LEAF_DEV - cap
    hub = jax.random.randint(jax.random.fold_in(key, 7919), (), 0, devices).astype(jnp.int32)

    def one_device(owner):
        sub_key = jax.random.fold_in(key, owner)
        first, second, third = jax.random.split(sub_key, 3)
        order = jax.random.permutation(first, far_count).astype(jnp.int32)
        hub_delta = ((hub - owner) % devices).astype(jnp.int32)
        remote = (hub_delta >= 4) & (hub_delta <= devices - 4)
        heavy = jnp.where(remote, hub_delta - 4, order[0]).astype(jnp.int32)
        slots = jnp.arange(far_count, dtype=jnp.int32)
        where_heavy = jnp.sum(jnp.where(order == heavy, slots, 0)).astype(jnp.int32)
        picks = (jnp.arange(spread_count, dtype=jnp.int32) % (far_count - 1)).astype(jnp.int32)
        picks = (picks + (picks >= where_heavy).astype(jnp.int32)).astype(jnp.int32)
        spread = order[picks]
        heavy_block = jnp.zeros((cap,), jnp.int32) + heavy
        far_deltas = (4 + jnp.concatenate([heavy_block, spread])).astype(jnp.int32)
        deltas = jnp.concatenate([near_deltas, far_deltas])
        deltas = jax.random.permutation(second, deltas).astype(jnp.int32)
        target = ((owner + deltas) % devices).astype(jnp.int32)
        within = jax.random.randint(third, (FAR_DEV,), 0, LEAF_DEV).astype(jnp.int32)
        return (target * LEAF_DEV + within).astype(jnp.int32)
    return jax.vmap(one_device)(jnp.arange(devices, dtype=jnp.int32)).reshape(FAR)


def touch_ends(result, rng, smallest, top_value):
    spot = [jax.random.randint(jax.random.fold_in(rng, axis), (), 0, length) for axis, length in enumerate(result.shape)]
    widest = result.shape.index(max(result.shape))
    beside = spot[:widest] + [(spot[widest] + 1) % result.shape[widest]] + spot[widest + 1:]
    return result.at[tuple(spot)].set(smallest).at[tuple(beside)].set(top_value)


def with_spikes(values, key, source, target, blocks, factor):
    owner, partner = [(jnp.arange(values.shape[dim]) // (values.shape[dim] // blocks)).reshape([-1 if axis == dim else 1 for axis in range(values.ndim)]) for dim in (source, target)]
    chosen = jax.random.permutation(key, blocks)[partner]
    strong = (owner == chosen) | (owner == (partner + blocks // 2) % blocks)
    return jnp.where(strong, factor * values, values)


def block_levels(rng, dims, pieces, smallest, high):
    level = 1.0
    for position, blocks in pieces:
        steps = jax.random.uniform(jax.random.fold_in(jax.random.fold_in(rng, 6), position), (blocks,), jnp.float32, smallest / len(pieces), high / len(pieces))
        level = level * jnp.repeat(jnp.exp(steps), dims[position] // blocks).reshape((-1,) + (1,) * (len(dims) - 1 - position))
    return level


def gaussian(stream_key, shape, scale, reach, cuts=(), held_as=jnp.bfloat16):
    drawn = jax.random.normal(stream_key, shape, jnp.float32) * scale
    if len(cuts) > 0:
        drawn = block_levels(stream_key, shape, cuts, -0.22, 0.18) * drawn
    return jnp.clip(drawn, min=-reach, max=reach).astype(held_as)


def heavy_noise(own_key, dims, scale, limit, shards, heavy, kind=jnp.bfloat16):
    result = scale * jax.random.normal(own_key, dims, jnp.float32)
    if shards:
        result = result * block_levels(own_key, dims, shards, -0.22, 0.18)
    return jnp.clip(with_spikes(result, jax.random.fold_in(own_key, 3), *heavy), -limit, limit).astype(kind)


def setup_inputs(seed: int = 0) -> dict:
    key_list = jax.random.split(jax.random.key(seed), 12)
    vectors = gaussian(key_list[0], (LEAVES, 2, LEAF), 1.0, 6.0, ((0, 128),))
    self_blocks = gaussian(key_list[1], (LEAVES, LEAF, LEAF), LEAF ** -0.5, 0.375, ((0, 128),))
    near_blocks = gaussian(key_list[2], (NEAR, LEAF, LEAF), LEAF ** -0.5, 0.375, ((0, 128),))
    near_row = touch_ends(jax.random.randint(key_list[3], (NEAR,), 0, LEAF_DEV), jax.random.fold_in(key_list[3], 1), 0, LEAF_DEV - 1).astype(jnp.int32)
    near_col = touch_ends(jax.random.randint(key_list[4], (NEAR,), 0, 2 * LEAF_DEV), jax.random.fold_in(key_list[4], 1), 0, (2 * LEAF_DEV) - 1).astype(jnp.int32)
    bases = gaussian(key_list[5], (LEAVES, LEAF, RANK), LEAF ** -0.5, 0.375, ((0, 128),))
    transfers = gaussian(key_list[6], (TRANS, RANK, RANK), (2 * RANK) ** -0.5, 0.5, ((0, 128),), jnp.float32)
    far_row = touch_ends(jax.random.randint(key_list[7], (FAR,), 0, LEAF_DEV), jax.random.fold_in(key_list[7], 1), 0, LEAF_DEV - 1).astype(jnp.int32)
    far_col = draw_far_col(jax.random.fold_in(key_list[11], 71), 0)
    couplings = gaussian(key_list[9], (FAR, RANK, RANK), RANK ** -0.5, 0.75, ((0, 128),), jnp.float32)
    root_couplings = heavy_noise(key_list[10], (N_SUB * N_LVL, N_SUB * N_LVL, RANK, RANK), (max(1, N_SUB * N_LVL * RANK // LEAF_DEV)) ** -0.5, 1.5, ((0, 128),), (1, 0, 128, 5.5), jnp.float32)
    return {"vectors": vectors, "self_blocks": self_blocks, "near_blocks": near_blocks, "near_row": near_row, "near_col": near_col, "bases": bases, "transfers": transfers, "far_row": far_row, "far_col": far_col, "couplings": couplings, "root_couplings": root_couplings}


HIGH = lax.Precision.HIGHEST


def tree_levels(count):
    levels = []
    offset = 0
    width = count
    while width > 1:
        levels.append((offset, width))
        offset += width
        width //= 2
    return levels


def tree_up(coeff, trans):
    for offset, width in tree_levels(coeff.shape[0]):
        prod = jnp.einsum('nvk,nkr->nvr', coeff, trans[offset:offset + width], precision=HIGH)
        coeff = prod.reshape(width // 2, 2, 2, prod.shape[-1]).sum(axis=1)
    return coeff[0]


def tree_down(top, leaf_terms, trans):
    field = top[None]
    for offset, width in reversed(tree_levels(leaf_terms.shape[0])):
        field = jnp.einsum('nkr,nvr->nvk', trans[offset:offset + width], jnp.repeat(field, 2, axis=0), precision=HIGH)
    return field + leaf_terms


def reference(vectors, self_blocks, near_blocks, near_row, near_col, bases, transfers, far_row, far_col, couplings, root_couplings):
    devices = N_SUB * N_LVL
    total = LEAF_DEV * devices
    xs = vectors.astype(jnp.float32)
    trans_dev = transfers.reshape(devices, 2 * LEAF_DEV - 2, RANK, RANK)

    def local_work(items):
        x_dev, self_dev, base_dev, trans_one = items
        self_out = jnp.einsum('lij,lvj->lvi', self_dev.astype(jnp.float32), x_dev, precision=HIGH)
        coeff = jnp.einsum('lvi,lik->lvk', x_dev, base_dev.astype(jnp.float32), precision=HIGH)
        return self_out, coeff, tree_up(coeff, trans_one)

    self_out, coeff, roots = lax.map(local_work, (xs.reshape(devices, LEAF_DEV, 2, LEAF), self_blocks.reshape(devices, LEAF_DEV, LEAF, LEAF), bases.reshape(devices, LEAF_DEV, LEAF, RANK), trans_dev))
    owner = (jnp.arange(NEAR, dtype=jnp.int32) // NEAR_DEV).astype(jnp.int32)
    row_leaf = (owner * LEAF_DEV + near_row).astype(jnp.int32)
    col_leaf = ((owner * LEAF_DEV + near_col) % total).astype(jnp.int32)

    def near_work(items):
        block, rows, cols = items
        block = block.astype(jnp.float32)
        forward = jnp.einsum('pij,pvj->pvi', block, xs[cols], precision=HIGH)
        backward = jnp.einsum('pij,pvi->pvj', block, xs[rows], precision=HIGH)
        return forward, backward

    forward, backward = lax.map(near_work, (near_blocks.reshape(devices, NEAR_DEV, LEAF, LEAF), row_leaf.reshape(devices, NEAR_DEV), col_leaf.reshape(devices, NEAR_DEV)))
    near_part = self_out.reshape(total, 2, LEAF)
    near_part = near_part.at[row_leaf].add(forward.reshape(NEAR, 2, LEAF))
    near_part = near_part.at[col_leaf].add(backward.reshape(NEAR, 2, LEAF))
    flat = coeff.reshape(total, 2, RANK)
    far_owner = (jnp.arange(FAR, dtype=jnp.int32) // FAR_DEV).astype(jnp.int32)
    far_rows = (far_owner * LEAF_DEV + far_row).astype(jnp.int32)
    far_forward = jnp.einsum('prk,pvk->pvr', couplings, flat[far_col], precision=HIGH)
    far_backward = jnp.einsum('prk,pvr->pvk', couplings, flat[far_rows], precision=HIGH)
    leaf_field = jnp.zeros((total, 2, RANK), jnp.float32).at[far_rows].add(far_forward).at[far_col].add(far_backward)
    root_field = jnp.einsum('derk,evk->dvr', root_couplings, roots, precision=HIGH)

    def down_work(items):
        top, terms, trans_one = items
        return tree_down(top, terms, trans_one)

    field = lax.map(down_work, (root_field, leaf_field.reshape(devices, LEAF_DEV, 2, RANK), trans_dev))
    field = field.reshape(total, 2, RANK).astype(jnp.bfloat16)
    far_part = jnp.einsum('lik,lvk->lvi', bases.astype(jnp.float32), field.astype(jnp.float32), precision=HIGH)
    return near_part + far_part
```

```python
import jax
import jax.numpy as jnp
from jax import lax
from jax.experimental import pallas as pl
from jax.experimental.pallas import tpu as pltpu
from jax.sharding import PartitionSpec as P

F32 = jnp.float32
BF16 = jnp.bfloat16
MESH = pl.DeviceIdType.MESH
OFFSETS = (-3, -2, -1, 1, 2, 3)
LEVELS = ((0, 32), (32, 16), (48, 8), (56, 4), (60, 2))


def dot(a, b, ca, cb):
    return lax.dot_general(a, b, (((ca,), (cb,)), ((), ())), preferred_element_type=F32)


def nn(a, b):
    return dot(a, b, 1, 0)


def nt(a, b):
    return dot(a, b, 1, 1)


def tn(a, b):
    return dot(a, b, 0, 0)


def split(x):
    hi = x.astype(BF16)
    return hi, (x - hi.astype(F32)).astype(BF16)


def pick(one_hot, x):
    hi, lo = split(x)
    return nn(one_hot, hi) + nn(one_hot, lo)


def iota(shape, dim):
    return lax.broadcasted_iota(jnp.int32, shape, dim)


def doubled(flat):
    turned = pltpu.roll(flat, 64, 1)
    low = iota(flat.shape, 1) < 64
    return jnp.where(low, flat, turned), jnp.where(low, turned, flat)


def spread(rows, blocks):
    row = iota((16, 128), 0) % 8
    half = iota((16, 128), 1) // 64
    return jnp.concatenate(
        [jnp.where(row == 2 * t + half, rows, 0.0) for t in range(blocks // 2)], axis=1
    )


def collect(wide, blocks):
    row = iota((16, 128), 0) % 8
    half = iota((16, 128), 1) // 64
    total = jnp.zeros((16, 128), F32)
    for t in range(blocks // 2):
        total = total + jnp.where(row == 2 * t + half, wide[:, 128 * t : 128 * t + 128], 0.0)
    return total + pltpu.roll(total, 64, 1)


def joined(rows):
    return jnp.concatenate([rows[0:8, 0:64], rows[8:16, 0:64]], axis=1)


def tree_up(cs, ps, trans):
    for offset, width in LEVELS:
        count = min(width, 8)
        for g in range(width // count):
            d0, d1 = doubled(cs[8 * g : 8 * g + 8, :])
            lh, ll = split(spread(jnp.concatenate([d0, d1], axis=0), count))
            e = trans[offset + 8 * g : offset + 8 * g + count].reshape(64 * count, 64)
            eh, el = split(e)
            ps[8 * g : 8 * g + 8, :] = joined(nn(lh, eh) + nn(ll, eh) + nn(lh, el))
        half = width // 2
        cs[0:half, :] = ps[pl.ds(0, half, stride=2), :] + ps[pl.ds(1, half, stride=2), :]


def tree_down(fs, trans):
    for offset, width in reversed(LEVELS):
        count = min(width, 8)
        groups = []
        for g in range(width // count):
            f = jnp.concatenate([fs[0, 8 * g : 8 * g + 8, :], fs[1, 8 * g : 8 * g + 8, :]], axis=0)
            fh, fl = split(f[:, 0:64])
            e = trans[offset + 8 * g : offset + 8 * g + count].reshape(64 * count, 64)
            eh, el = split(e)
            groups.append(collect(nt(fh, eh) + nt(fl, eh) + nt(fh, el), count))
        for g, child in enumerate(groups):
            for v in range(2):
                if offset == 0:
                    fs[v, 8 * g : 8 * g + 8, :] = child[8 * v : 8 * v + 8]
                else:
                    fs[v, pl.ds(16 * g, 8, stride=2), :] = child[8 * v : 8 * v + 8]
                    fs[v, pl.ds(16 * g + 1, 8, stride=2), :] = child[8 * v : 8 * v + 8]


def kernel(
    vec, near_row, near_col, far_row, far_col,
    self_h, near_h, base_h, trans_h, coup_h, root_h,
    out,
    selfs, nears, bases, trans, coup, roots,
    x32, xs, xn, cs, ps, fs, coupb, bwd, fwd, leaf, nearp, nwork, back, backin,
    ga, gb, gc, gcin, nsend, nrecv,
    load_sem, a_send, a_recv, b_send, b_recv, c_send, c_recv, o_send, o_recv,
):
    s = lax.axis_index("sub")
    y = lax.axis_index("lvl")
    z = lax.div(s, 8)
    x = lax.rem(lax.div(s, 2), 4)
    c = lax.rem(s, 2)
    me = s * 4 + y

    loads = []
    for i, (src, dst) in enumerate(
        ((base_h, bases), (coup_h, coup), (trans_h, trans), (self_h, selfs), (near_h, nears), (root_h, roots))
    ):
        load = pltpu.make_async_copy(src, dst, load_sem.at[i])
        load.start()
        loads.append(load)

    def along(dim, o):
        if dim == "y":
            return s, lax.rem(y + o, 4)
        if dim == "x":
            return (z * 4 + lax.rem(x + o, 4)) * 2 + c, y
        return (lax.rem(z + o, 4) * 4 + x) * 2 + c, y

    sibling = ((z * 4 + x) * 2 + 1 - c, y)

    def shifted(o):
        m = lax.rem(me + o + 128, 128)
        return lax.div(m, 4), lax.rem(m, 4)

    barrier = pltpu.get_barrier_semaphore()
    peers = [along(d, o) for d in "xyz" for o in (1, 2, 3)] + [sibling] + [shifted(o) for o in OFFSETS]
    for peer in peers:
        pl.semaphore_signal(barrier, inc=1, device_id=peer, device_id_type=MESH)

    pending = []

    def send(src, dst, ssem, rsem, peer):
        copy = pltpu.make_async_remote_copy(
            src_ref=src, dst_ref=dst, send_sem=ssem, recv_sem=rsem, device_id=peer, device_id_type=MESH
        )
        copy.start()
        pending.append(copy)

    def arrive(dst, ssem, rsem):
        pltpu.make_async_remote_copy(
            src_ref=dst, dst_ref=dst, send_sem=ssem, recv_sem=rsem, device_id=sibling, device_id_type=MESH
        ).wait_recv()

    place = {"x": x, "y": y, "z": z}

    class Stream:
        def __init__(self, ref, order, ssem, rsem):
            self.ref, self.ssem, self.rsem = ref, ssem, rsem
            self.dims = order
            self.f, self.s, self.t = (place[d] for d in order)

        def chunk(self, phase, o):
            if phase == 0:
                return self.ref.at[c, self.t, self.s, lax.rem(self.f + 4 - o, 4)]
            if phase == 1:
                return self.ref.at[c, self.t, lax.rem(self.s + 4 - o, 4)]
            return self.ref.at[c, lax.rem(self.t + 4 - o, 4)]

        def push(self, phase):
            mine = self.chunk(phase, 0)
            for o in (1, 2, 3):
                k = 3 * phase + o - 1
                send(mine, mine, self.ssem.at[k], self.rsem.at[k], along(self.dims[phase], o))
            if phase == 2:
                self.over(0)

        def pull(self, phase, o):
            k = 3 * phase + o - 1
            arrive(self.chunk(phase, o), self.ssem.at[k], self.rsem.at[k])

        def over(self, o):
            mine = self.chunk(2, o)
            send(mine, mine, self.ssem.at[9 + o], self.rsem.at[9 + o], sibling)

        def pull_over(self, o):
            k = 9 + o
            dst = self.ref.at[1 - c, lax.rem(self.t + 4 - o, 4)]
            arrive(dst, self.ssem.at[k], self.rsem.at[k])

        def pull_all(self, phase):
            for o in (1, 2, 3):
                self.pull(phase, o)
                if phase == 2:
                    self.over(o)

    sa = Stream(ga, "zxy", a_send, a_recv)
    sb = Stream(gb, "yxz", b_send, b_recv)
    sc = Stream(gc, "yxz", c_send, c_recv)

    for v in range(2):
        xv = vec[:, v, :].astype(F32)
        x32[v, 0:32, :] = xv
        xs[v] = xv.astype(BF16)

    row16 = iota((16, 256), 0) % 8
    far_r = far_row[...]
    far_c = far_col[...]
    own_hot = (iota((32, 128), 0) == far_r).astype(BF16)

    loads[0].wait()

    def coeff_group(g, carry):
        xg = jnp.concatenate([x32[0, pl.ds(8 * g, 8), :], x32[1, pl.ds(8 * g, 8), :]], axis=0)
        lhs = jnp.concatenate([jnp.where(row16 == j, xg, 0.0).astype(BF16) for j in range(8)], axis=1)
        cs[pl.ds(8 * g, 8), :] = joined(nn(lhs, bases[pl.ds(8 * g, 8)].reshape(2048, 64)))
        return carry

    lax.fori_loop(0, 4, coeff_group, 0)
    cb = cs[...].astype(BF16)
    ga[c, y, x, z] = cb
    pl.semaphore_wait(barrier, len(peers))
    sa.push(0)
    send(xs, xn, o_send.at[0], o_recv.at[0], shifted(-1))

    ch, cl = split(cs[...])
    d0, d1 = doubled(tn(own_hot, ch) + tn(own_hot, cl))
    bwd[0] = d0
    bwd[1] = d1
    loads[1].wait()

    def back_group(g, carry):
        rows = jnp.concatenate([bwd[0, pl.ds(8 * g, 8), :], bwd[1, pl.ds(8 * g, 8), :]], axis=0)
        wh, wl = split(coup[pl.ds(8 * g, 8)].reshape(512, 64))
        coupb[0, pl.ds(8 * g, 8)] = wh.reshape(8, 64, 64)
        coupb[1, pl.ds(8 * g, 8)] = wl.reshape(8, 64, 64)
        lh, ll = split(spread(rows, 8))
        fwd[pl.ds(8 * g, 8), :] = joined(nn(lh, wh) + nn(ll, wh) + nn(lh, wl))
        return carry

    lax.fori_loop(0, 16, back_group, 0)
    bh, bl = split(fwd[...])
    dev = far_c // 32
    dist = (dev - me + 128) % 128
    is_far = (dist > 3) & (dist < 125)
    before = (iota((128, 128), 0) < iota((128, 128), 1)).astype(BF16)
    pos = nn(jnp.broadcast_to(is_far.astype(F32), (16, 128)).astype(BF16), before)[0:1, :].astype(jnp.int32)
    pos = jnp.where(is_far, pos, -1000)
    far_hot = (iota((32, 128), 0) == pos).astype(BF16)
    gb[c, z, x, y] = nn(far_hot, bh).astype(BF16)
    sb.push(0)
    leaf_of = iota((32, 128), 0)
    near_hot = jnp.concatenate(
        [(leaf_of + ((me + o + 128) % 128) * 32 == far_c).astype(BF16) for o in OFFSETS], axis=0
    )
    nsend[...] = (nn(near_hot, bh) + nn(near_hot, bl)).astype(BF16).reshape(6, 32, 128)
    for i, o in enumerate(OFFSETS):
        send(nsend.at[i], nrecv.at[i], o_send.at[2 + i], o_recv.at[2 + i], shifted(o))

    for o in (1, 2, 3):
        sa.pull(0, o)
    sa.push(1)

    loads[2].wait()
    tree_up(cs, ps, trans)
    rh, rl = split(cs[0:1, :])
    lane_hot = (iota((128, 128), 0) == pos + 32 * y).astype(BF16)
    row_id = iota((16, 128), 0)
    codes = jnp.where(row_id == 0, dev, jnp.where(row_id == 1, far_c - dev * 32, 0)).astype(F32).astype(BF16)
    tile = nt(codes, lane_hot)
    tile = jnp.where(row_id == 4 + 2 * y, rh.astype(F32), tile)
    tile = jnp.where(row_id == 5 + 2 * y, rl.astype(F32), tile)
    gcin[y] = tile.astype(BF16)
    for o in (1, 2, 3):
        send(gcin.at[y], gcin.at[y], c_send.at[o - 1], c_recv.at[o - 1], along("y", o))

    sa.pull_all(1)
    sa.push(2)
    sb.pull_all(0)
    sb.push(1)
    for o in (1, 2, 3):
        arrive(gcin.at[lax.rem(y + 4 - o, 4)], c_send.at[o - 1], c_recv.at[o - 1])
    merged = gcin[0].astype(F32) + gcin[1].astype(F32) + gcin[2].astype(F32) + gcin[3].astype(F32)
    gc[c, z, x] = merged.astype(BF16)
    for o in (1, 2, 3):
        send(gc.at[c, z, x], gc.at[c, z, x], c_send.at[2 + o], c_recv.at[2 + o], along("x", o))

    def group_rows(ref, g):
        return jnp.concatenate([ref[0, pl.ds(8 * g, 8), :], ref[1, pl.ds(8 * g, 8), :]], axis=0)

    def run_blocks(src, dst, blocks, product, add):
        def body(g, carry):
            rows = group_rows(src, g)
            acc = jnp.zeros((16, 256), F32)
            for j in range(8):
                acc = acc + product(jnp.where(row16 == j, rows, 0.0).astype(BF16), blocks[8 * g + j])
            for v in range(2):
                part = acc[8 * v : 8 * v + 8]
                if add:
                    part = part + dst[v, pl.ds(8 * g, 8), :]
                dst[v, pl.ds(8 * g, 8), :] = part
            return carry

        lax.fori_loop(0, 4, body, 0)

    loads[3].wait()
    run_blocks(x32, nearp, selfs, nt, False)

    sb.pull_all(1)
    sb.push(2)
    for o in (1, 2, 3):
        arrive(gc.at[c, z, lax.rem(x + 4 - o, 4)], c_send.at[2 + o], c_recv.at[2 + o])
    for o in (1, 2, 3):
        send(gc.at[c, z], gc.at[c, z], c_send.at[5 + o], c_recv.at[5 + o], along("z", o))
    sc.over(0)
    sa.pull_all(2)

    row_hot = (iota((32, 32), 0) == near_row[...]).astype(BF16)
    col_hot = (iota((64, 32), 0) == near_col[...]).astype(BF16)
    for v in range(2):
        nwork[v] = tn(row_hot, xs[v])
    loads[4].wait()
    run_blocks(nwork, nwork, nears, nn, False)
    for v in range(2):
        both = pick(col_hot, nwork[v])
        nearp[v] = nearp[v] + both[0:32]
        back[v] = both[32:64]
    send(back, backin, o_send.at[1], o_recv.at[1], shifted(1))

    sc.pull_all(2)
    sb.pull_all(2)

    arrive(xn, o_send.at[0], o_recv.at[0])
    for v in range(2):
        nwork[v] = tn(col_hot, jnp.concatenate([xs[v], xn[v]], axis=0))
    run_blocks(nwork, nwork, nears, nt, False)
    for v in range(2):
        nearp[v] = nearp[v] + pick(row_hot, nwork[v])

    for o in range(4):
        sc.pull_over(o)
    loads[5].wait()

    def root_group(i, carry):
        acc0, acc1 = carry
        t = gc[lax.rem(i, 2), lax.div(i, 8), lax.rem(lax.div(i, 2), 4)].astype(F32)
        turned = pltpu.roll(t, 64, 1)
        for k in range(4):
            m = roots[0, 4 * i + k]
            acc0 = acc0 + m * (t[4 + 2 * k : 5 + 2 * k, 0:64] + t[5 + 2 * k : 6 + 2 * k, 0:64])
            acc1 = acc1 + m * (turned[4 + 2 * k : 5 + 2 * k, 0:64] + turned[5 + 2 * k : 6 + 2 * k, 0:64])
        return acc0, acc1

    zero = jnp.zeros((64, 64), F32)
    tops = lax.fori_loop(0, 32, root_group, (zero, zero))
    ones = jnp.ones((16, 64), BF16)
    for v in range(2):
        th, tl = split(tops[v])
        top = (nt(ones, th) + nt(ones, tl))[0:8]
        fs[v, 0:8, :] = jnp.concatenate([top, top], axis=1)
    tree_down(fs, trans)

    for o in range(4):
        sa.pull_over(o)
    ldev = far_c // 32
    perm = ((ldev // 4) % 2) * 64 + (ldev % 4) * 16 + ((ldev // 8) % 4) * 4 + ldev // 32
    code = (perm * 32 + far_c - ldev * 32).astype(F32)
    codes_q = jnp.transpose(jnp.broadcast_to(code, (128, 128)))
    lane = iota((128, 128), 1).astype(F32)
    partner = jnp.zeros((128, 128), F32)
    for i in range(8):
        for j in range(4):
            base = float(128 * (i * 4 + j))
            hot = (codes_q == lane + base).astype(BF16)
            partner = partner + nn(hot, ga[i // 4, i % 4, j].reshape(128, 128))
    bwd[0] = partner
    bwd[1] = pltpu.roll(partner, 64, 1)

    def fwd_group(g, carry):
        rows = group_rows(bwd, g)[:, 0:64].astype(BF16)
        wide = nt(rows, coupb[0, pl.ds(8 * g, 8)].reshape(512, 64))
        wide = wide + nt(rows, coupb[1, pl.ds(8 * g, 8)].reshape(512, 64))
        r = collect(wide, 8)
        fwd[pl.ds(8 * g, 8), :] = jnp.where(iota((8, 128), 1) < 64, r[0:8], r[8:16])
        return carry

    lax.fori_loop(0, 16, fwd_group, 0)
    acc = pick(own_hot, fwd[...])

    for o in range(4):
        sb.pull_over(o)

    for i in range(2):
        for j in range(4):
            for k in range(4):
                t = gc[i, j, k].astype(F32)
                hot = ((t[0:1, :] == me.astype(F32)) & (t[1:2, :] == leaf_of.astype(F32))).astype(BF16)
                acc = acc + nn(hot, gb[i, j, k].reshape(128, 128))
    for i in range(6):
        arrive(nrecv.at[i], o_send.at[2 + i], o_recv.at[2 + i])
        acc = acc + nrecv[i].astype(F32)

    field = acc + jnp.where(iota((32, 128), 1) < 64, fs[0], fs[1])
    d0, d1 = doubled(field.astype(BF16).astype(F32))
    fs[0] = d0
    fs[1] = d1
    arrive(backin, o_send.at[1], o_recv.at[1])

    def out_group(g, carry):
        rows = group_rows(fs, g)[:, 0:64]
        acc = jnp.zeros((16, 256), F32)
        mask = iota((16, 64), 0) % 8
        for j in range(8):
            acc = acc + nt(jnp.where(mask == j, rows, 0.0).astype(BF16), bases[8 * g + j])
        for v in range(2):
            here = pl.ds(8 * g, 8)
            out[v, here, :] = acc[8 * v : 8 * v + 8] + nearp[v, here, :] + backin[v, here, :]
        return carry

    lax.fori_loop(0, 4, out_group, 0)
    for copy in pending:
        copy.wait_send()


def shards(
    vectors, self_blocks, near_blocks, near_row, near_col, bases, transfers, far_row, far_col, couplings,
    root_couplings,
):
    vmem = pl.BlockSpec(memory_space=pltpu.VMEM)
    hbm = pl.BlockSpec(memory_space=pl.ANY)
    result = pl.pallas_call(
        kernel,
        out_shape=jax.ShapeDtypeStruct((2, 32, 256), F32),
        in_specs=[vmem] * 5 + [hbm] * 6,
        out_specs=vmem,
        scratch_shapes=[
            pltpu.VMEM((32, 256, 256), BF16),
            pltpu.VMEM((32, 256, 256), BF16),
            pltpu.VMEM((32, 256, 64), BF16),
            pltpu.VMEM((62, 64, 64), F32),
            pltpu.VMEM((128, 64, 64), F32),
            pltpu.VMEM((1, 128, 64, 64), F32),
            pltpu.VMEM((2, 32, 256), F32),
            pltpu.VMEM((2, 32, 256), BF16),
            pltpu.VMEM((2, 32, 256), BF16),
            pltpu.VMEM((32, 128), F32),
            pltpu.VMEM((32, 128), F32),
            pltpu.VMEM((2, 32, 128), F32),
            pltpu.VMEM((2, 128, 64, 64), BF16),
            pltpu.VMEM((2, 128, 128), F32),
            pltpu.VMEM((128, 128), F32),
            pltpu.VMEM((32, 128), F32),
            pltpu.VMEM((2, 32, 256), F32),
            pltpu.VMEM((2, 32, 256), F32),
            pltpu.VMEM((2, 32, 256), F32),
            pltpu.VMEM((2, 32, 256), F32),
            pltpu.VMEM((2, 4, 4, 4, 32, 128), BF16),
            pltpu.VMEM((2, 4, 4, 4, 32, 128), BF16),
            pltpu.VMEM((2, 4, 4, 16, 128), BF16),
            pltpu.VMEM((4, 16, 128), BF16),
            pltpu.VMEM((6, 32, 128), BF16),
            pltpu.VMEM((6, 32, 128), BF16),
            pltpu.SemaphoreType.DMA((6,)),
            pltpu.SemaphoreType.DMA((13,)),
            pltpu.SemaphoreType.DMA((13,)),
            pltpu.SemaphoreType.DMA((13,)),
            pltpu.SemaphoreType.DMA((13,)),
            pltpu.SemaphoreType.DMA((13,)),
            pltpu.SemaphoreType.DMA((13,)),
            pltpu.SemaphoreType.DMA((8,)),
            pltpu.SemaphoreType.DMA((8,)),
        ],
        compiler_params=pltpu.CompilerParams(
            collective_id=0, has_side_effects=True, vmem_limit_bytes=50 * 1024 * 1024
        ),
    )(
        vectors, near_row.reshape(1, 32), near_col.reshape(1, 32), far_row.reshape(1, 128), far_col.reshape(1, 128),
        self_blocks, near_blocks, bases, transfers, couplings, root_couplings,
    )
    return result.transpose(1, 0, 2)


def solution(mesh):
    both = ("sub", "lvl")
    in_specs = (
        P(both, None, None), P(both, None, None), P(both, None, None), P(both), P(both), P(both, None, None),
        P(both, None, None), P(both), P(both), P(both, None, None), P(both, None, None, None),
    )
    return jax.shard_map(shards, mesh=mesh, in_specs=in_specs, out_specs=P(both, None, None), check_vma=False)
```

```python
import jax
import jax.numpy as jnp
from jax import lax
from jax.experimental import pallas as pl
from jax.experimental.pallas import tpu as pltpu
from jax.sharding import PartitionSpec as P

F32 = jnp.float32
BF16 = jnp.bfloat16
MESH = pl.DeviceIdType.MESH
OFFSETS = (-3, -2, -1, 1, 2, 3)
LEVELS = ((0, 32), (32, 16), (48, 8), (56, 4), (60, 2))


def dot(a, b, ca, cb):
    return lax.dot_general(a, b, (((ca,), (cb,)), ((), ())), preferred_element_type=F32)


def nn(a, b):
    return dot(a, b, 1, 0)


def nt(a, b):
    return dot(a, b, 1, 1)


def tn(a, b):
    return dot(a, b, 0, 0)


def split(x):
    hi = x.astype(BF16)
    return hi, (x - hi.astype(F32)).astype(BF16)


def pick(one_hot, x):
    hi, lo = split(x)
    return nn(one_hot, hi) + nn(one_hot, lo)


def iota(shape, dim):
    return lax.broadcasted_iota(jnp.int32, shape, dim)


def doubled(flat):
    turned = pltpu.roll(flat, 64, 1)
    low = iota(flat.shape, 1) < 64
    return jnp.where(low, flat, turned), jnp.where(low, turned, flat)


def spread(rows, blocks):
    row = iota((16, 128), 0) % 8
    half = iota((16, 128), 1) // 64
    return jnp.concatenate(
        [jnp.where(row == 2 * t + half, rows, 0.0) for t in range(blocks // 2)], axis=1
    )


def collect(wide, blocks):
    row = iota((16, 128), 0) % 8
    half = iota((16, 128), 1) // 64
    total = jnp.zeros((16, 128), F32)
    for t in range(blocks // 2):
        total = total + jnp.where(row == 2 * t + half, wide[:, 128 * t : 128 * t + 128], 0.0)
    return total + pltpu.roll(total, 64, 1)


def joined(rows):
    return jnp.concatenate([rows[0:8, 0:64], rows[8:16, 0:64]], axis=1)


def abreast(rows):
    return jnp.where(iota((8, 128), 1) < 64, rows[0:8], rows[8:16])


def contract(mats, terms, dst):
    t = terms[...]

    def body(i, carry):
        for j in range(8):
            m = mats[8 * i + j]
            for v in range(2):
                row = jnp.sum(m * t[64 * v : 64 * v + 64], axis=0, keepdims=True)
                dst[pl.ds(64 * v + 8 * i + j, 1), :] = row
        return carry

    lax.fori_loop(0, 8, body, 0)


def contract_turned(mats, terms, dst):
    def body(i, carry):
        acc0, acc1 = carry
        for j in range(8):
            m = mats[8 * i + j]
            acc0 = acc0 + m * terms[pl.ds(8 * i + j, 1), :]
            acc1 = acc1 + m * terms[pl.ds(64 + 8 * i + j, 1), :]
        return acc0, acc1

    zero = jnp.zeros((64, 128), F32)
    acc0, acc1 = lax.fori_loop(0, 8, body, (zero, zero))
    dst[0:64, :] = acc0
    dst[64:128, :] = acc1


def tree_up(cs, ps, trans):
    for offset, width in LEVELS:
        count = min(width, 8)
        for g in range(width // count):
            d0, d1 = doubled(cs[8 * g : 8 * g + 8, :])
            lh, ll = split(spread(jnp.concatenate([d0, d1], axis=0), count))
            e = trans[offset + 8 * g : offset + 8 * g + count].reshape(64 * count, 64)
            eh, el = split(e)
            ps[8 * g : 8 * g + 8, :] = joined(nn(lh, eh) + nn(ll, eh) + nn(lh, el))
        half = width // 2
        cs[0:half, :] = ps[pl.ds(0, half, stride=2), :] + ps[pl.ds(1, half, stride=2), :]


def tree_down(fs, trans):
    for offset, width in reversed(LEVELS):
        count = min(width, 8)
        groups = []
        for g in range(width // count):
            f = jnp.concatenate([fs[0, 8 * g : 8 * g + 8, :], fs[1, 8 * g : 8 * g + 8, :]], axis=0)
            fh, fl = split(f[:, 0:64])
            e = trans[offset + 8 * g : offset + 8 * g + count].reshape(64 * count, 64)
            eh, el = split(e)
            groups.append(collect(nt(fh, eh) + nt(fl, eh) + nt(fh, el), count))
        for g, child in enumerate(groups):
            for v in range(2):
                if offset == 0:
                    fs[v, 8 * g : 8 * g + 8, :] = child[8 * v : 8 * v + 8]
                else:
                    fs[v, pl.ds(16 * g, 8, stride=2), :] = child[8 * v : 8 * v + 8]
                    fs[v, pl.ds(16 * g + 1, 8, stride=2), :] = child[8 * v : 8 * v + 8]


def kernel(
    vec_h, near_row_h, near_col_h, far_row_h, far_col_h,
    self_h, near_h, base_h, trans_h, coup_h, root_h,
    out,
    vec, near_row, near_col, far_row, far_col,
    selfs, nears, bases, trans, coup, roots,
    x32, xs, xn, cs, ps, fs, terms, sums, nearp, nwork, back, backin,
    ga, gb, gc, gcin, nsend, nrecv,
    load_sem, send_sem, a_recv, b_recv, c_recv, o_recv,
):
    s = lax.axis_index("sub")
    y = lax.axis_index("lvl")
    z = lax.div(s, 8)
    x = lax.rem(lax.div(s, 2), 4)
    c = lax.rem(s, 2)
    me = s * 4 + y

    loads = []
    for i, (src, dst) in enumerate(
        (
            (vec_h, vec), (far_row_h, far_row), (far_col_h, far_col), (near_row_h, near_row), (near_col_h, near_col),
            (base_h, bases), (coup_h, coup), (trans_h, trans), (self_h, selfs), (near_h, nears), (root_h, roots),
        )
    ):
        load = pltpu.make_async_copy(src, dst, load_sem.at[i])
        load.start()
        loads.append(load)

    def at(x=0, y=0, z=0):
        ox, oy, oz = x, y, z
        return (
            (lax.rem(place["z"] + oz, 4) * 4 + lax.rem(place["x"] + ox, 4)) * 2 + c,
            lax.rem(place["y"] + oy, 4),
        )

    place = {"x": x, "y": y, "z": z}
    sibling = ((z * 4 + x) * 2 + 1 - c, y)

    def shifted(o):
        m = lax.rem(me + o + 128, 128)
        return lax.div(m, 4), lax.rem(m, 4)

    barrier = pltpu.get_barrier_semaphore()
    peers = [
        at(i, j, k)
        for i in range(4)
        for j in range(4)
        for k in range(4)
        if 0 < (i > 0) + (j > 0) + (k > 0) < 3
    ]
    peers = peers + [sibling] + [shifted(o) for o in OFFSETS]
    for peer in peers:
        pl.semaphore_signal(barrier, inc=1, device_id=peer, device_id_type=MESH)

    pending = []

    def send(src, dst, rsem, peer):
        copy = pltpu.make_async_remote_copy(
            src_ref=src, dst_ref=dst, send_sem=send_sem.at[len(pending)], recv_sem=rsem,
            device_id=peer, device_id_type=MESH,
        )
        copy.start()
        pending.append(copy)

    def arrive(dst, rsem):
        pltpu.make_async_remote_copy(
            src_ref=dst, dst_ref=dst, send_sem=send_sem.at[0], recv_sem=rsem,
            device_id=sibling, device_id_type=MESH,
        ).wait_recv()

    class Stream:
        def __init__(self, ref, order, rsem):
            self.ref, self.rsem, self.dims = ref, rsem, order
            self.f, self.s, self.t = (place[d] for d in order)

        def behind(self, index, o):
            return lax.rem(index + 4 - o, 4)

        def spread(self):
            mine = self.ref.at[c, self.t, self.s, self.f]
            for i in (2, 1, 3, 0):
                for j in (2, 1, 3, 0):
                    if i or j:
                        k = 4 * i + (j if i == 0 else 0)
                        send(mine, mine, self.rsem.at[k], at(**{self.dims[1]: i, self.dims[0]: j}))

        def relay(self, i):
            if i == 0:
                for j in (1, 2, 3):
                    arrive(self.ref.at[c, self.t, self.s, self.behind(self.f, j)], self.rsem.at[j])
            else:
                arrive(self.ref.at[c, self.t, self.behind(self.s, i)], self.rsem.at[4 * i])
            row = self.ref.at[c, self.t, self.behind(self.s, i)]
            for o in (2, 1, 3):
                send(row, row, self.rsem.at[16 + 4 * o + i], at(**{self.dims[2]: o}))

        def take(self, o):
            if o:
                for i in range(4):
                    arrive(self.ref.at[c, self.behind(self.t, o), self.behind(self.s, i)], self.rsem.at[16 + 4 * o + i])
            plane = self.ref.at[c, self.behind(self.t, o)]
            send(plane, plane, self.rsem.at[32 + o], sibling)
            return c, self.behind(self.t, o)

        def take_other(self, o):
            arrive(self.ref.at[1 - c, self.behind(self.t, o)], self.rsem.at[32 + o])
            return 1 - c, self.behind(self.t, o)

    sa = Stream(ga, "yxz", a_recv)
    sb = Stream(gb, "yzx", b_recv)

    for i in range(5):
        loads[i].wait()
    for v in range(2):
        xv = vec[:, v, :].astype(F32)
        x32[v, 0:32, :] = xv
        xs[v] = xv.astype(BF16)

    row16 = iota((16, 256), 0) % 8
    far_r = far_row[...]
    far_c = far_col[...]
    own_hot = (iota((32, 128), 0) == far_r).astype(BF16)

    def group_rows(ref, g):
        return jnp.concatenate([ref[0, pl.ds(8 * g, 8), :], ref[1, pl.ds(8 * g, 8), :]], axis=0)

    loads[5].wait()

    def coeff_group(g, carry):
        wide = nt(group_rows(x32, g).astype(BF16), bases[pl.ds(8 * g, 8)].reshape(512, 256))
        cs[pl.ds(8 * g, 8), :] = abreast(collect(wide, 8))
        return carry

    lax.fori_loop(0, 4, coeff_group, 0)
    ch, cl = split(cs[...])
    ga[c, z, x, y] = ch

    terms[...] = tn(ch, own_hot) + tn(cl, own_hot)
    loads[6].wait()
    contract_turned(coup, terms, sums)
    bh, bl = split(sums[...])
    dev = far_c // 32
    dist = (dev - me + 128) % 128
    is_far = (dist > 3) & (dist < 125)
    before = (iota((128, 128), 0) < iota((128, 128), 1)).astype(BF16)
    pos = nn(jnp.broadcast_to(is_far.astype(F32), (16, 128)).astype(BF16), before)[0:1, :].astype(jnp.int32)
    pos = jnp.where(is_far, pos, -1000)
    far_hot = (iota((32, 128), 0) == pos).astype(BF16)
    gb[c, x, z, y] = nt(far_hot, bh).astype(BF16)
    leaf_of = iota((32, 128), 0)
    near_hot = jnp.concatenate(
        [(leaf_of + ((me + o + 128) % 128) * 32 == far_c).astype(BF16) for o in OFFSETS], axis=0
    )
    nsend[...] = (nt(near_hot, bh) + nt(near_hot, bl)).astype(BF16).reshape(6, 32, 128)

    loads[7].wait()
    tree_up(cs, ps, trans)
    rh, rl = split(cs[0:1, :])
    lane_hot = (iota((128, 128), 0) == pos + 32 * y).astype(BF16)
    row_id = iota((16, 128), 0)
    codes = jnp.where(row_id == 0, dev, jnp.where(row_id == 1, far_c - dev * 32, 0)).astype(F32).astype(BF16)
    tile = nt(codes, lane_hot)
    tile = jnp.where(row_id == 4 + 2 * y, rh.astype(F32), tile)
    tile = jnp.where(row_id == 5 + 2 * y, rl.astype(F32), tile)
    gcin[y] = tile.astype(BF16)

    pl.semaphore_wait(barrier, len(peers))
    sa.spread()
    sb.spread()
    for o in (1, 2, 3):
        send(gcin.at[y], gcin.at[y], c_recv.at[o], at(y=o))
    send(xs, xn, o_recv.at[0], shifted(-1))
    for i, o in enumerate(OFFSETS):
        send(nsend.at[i], nrecv.at[i], o_recv.at[2 + i], shifted(o))

    def run_blocks(src, dst, blocks, product):
        def body(g, carry):
            rows = group_rows(src, g)
            acc = jnp.zeros((16, 256), F32)
            for j in range(8):
                acc = acc + product(jnp.where(row16 == j, rows, 0.0).astype(BF16), blocks[8 * g + j])
            for v in range(2):
                dst[v, pl.ds(8 * g, 8), :] = acc[8 * v : 8 * v + 8]
            return carry

        lax.fori_loop(0, 4, body, 0)

    loads[8].wait()
    run_blocks(x32, nearp, selfs, nt)

    row_hot = (iota((32, 32), 0) == near_row[...]).astype(BF16)
    col_hot = (iota((64, 32), 0) == near_col[...]).astype(BF16)
    for v in range(2):
        nwork[v] = tn(row_hot, xs[v])
    loads[9].wait()
    run_blocks(nwork, nwork, nears, nn)
    for v in range(2):
        both = pick(col_hot, nwork[v])
        nearp[v] = nearp[v] + both[0:32]
        back[v] = both[32:64]
    send(back, backin, o_recv.at[1], shifted(1))

    sa.relay(0)
    sb.relay(0)
    for o in (1, 2, 3):
        arrive(gcin.at[lax.rem(y + 4 - o, 4)], c_recv.at[o])
    merged = gcin[0].astype(F32) + gcin[1].astype(F32) + gcin[2].astype(F32) + gcin[3].astype(F32)
    gc[c, z, x] = merged.astype(BF16)
    for i in (2, 1, 3, 0):
        for j in (2, 1, 3, 0):
            if i or j:
                k = 4 + 4 * i + (j if i == 0 else 0)
                send(gc.at[c, z, x], gc.at[c, z, x], c_recv.at[k], at(z=i, x=j))
    for i in (1, 3, 2):
        sa.relay(i)
        sb.relay(i)

    arrive(xn, o_recv.at[0])
    for v in range(2):
        nwork[v] = tn(col_hot, jnp.concatenate([xs[v], xn[v]], axis=0))
    run_blocks(nwork, nwork, nears, nt)
    for v in range(2):
        nearp[v] = nearp[v] + pick(row_hot, nwork[v])

    ldev = far_c // 32
    perm = ((ldev // 4) % 2) * 64 + (ldev // 32) * 16 + ((ldev // 8) % 4) * 4 + ldev % 4
    code = (perm * 32 + far_c - ldev * 32).astype(F32)
    codes_q = jnp.transpose(jnp.broadcast_to(code, (128, 128)))
    lane = iota((128, 128), 1).astype(F32)

    def gather(place_a, partner):
        i, j = place_a
        for k in range(4):
            base = (((i * 4 + j) * 4 + k) * 128).astype(F32)
            partner = partner + nn((codes_q == lane + base).astype(BF16), ga[i, j, k].reshape(128, 128))
        return partner

    sa.take(0)
    sb.take(0)
    for i in range(4):
        if i:
            arrive(gc.at[c, lax.rem(z + 4 - i, 4)], c_recv.at[4 + 4 * i])
        else:
            for j in (1, 2, 3):
                arrive(gc.at[c, z, lax.rem(x + 4 - j, 4)], c_recv.at[4 + j])
    send(gc.at[c], gc.at[c], c_recv.at[0], sibling)
    partner = gather((c, z), jnp.zeros((128, 128), F32))
    for o in (1, 3, 2):
        where = sa.take(o)
        sb.take(o)
        partner = gather(where, partner)

    arrive(gc.at[1 - c], c_recv.at[0])
    row_at = iota((128, 512), 1)
    tile_at = row_at // 16
    line = row_at % 16
    holder = (((tile_at // 4) % 4 * 4 + tile_at % 4) * 2 + tile_at // 16) * 4 + (line - 4) // 2
    sel = ((holder == iota((128, 512), 0)) & (line >= 4) & (line < 12)).astype(BF16)
    terms[...] = jnp.transpose(nn(sel, gc[...].reshape(512, 128)))
    loads[10].wait()
    contract(roots, terms, sums)
    sh, sl = split(sums[...])
    ones = jnp.ones((16, 128), BF16)
    top = (nt(ones, sh) + nt(ones, sl))[0:8]
    d0, d1 = doubled(top)
    fs[0, 0:8, :] = d0
    fs[1, 0:8, :] = d1
    tree_down(fs, trans)

    for o in (0, 1, 3, 2):
        partner = gather(sa.take_other(o), partner)
    terms[...] = jnp.transpose(partner)
    contract(coup, terms, sums)
    sh, sl = split(sums[...])
    acc = nt(own_hot, sh) + nt(own_hot, sl)

    def deliver(place_b, acc):
        i, j = place_b
        for k in range(4):
            t = gc[i, k, j].astype(F32)
            hot = ((t[0:1, :] == me.astype(F32)) & (t[1:2, :] == leaf_of.astype(F32))).astype(BF16)
            acc = acc + nn(hot, gb[i, j, k].reshape(128, 128))
        return acc

    for o in range(4):
        acc = deliver((c, lax.rem(x + 4 - o, 4)), acc)
    for i in range(6):
        arrive(nrecv.at[i], o_recv.at[2 + i])
        acc = acc + nrecv[i].astype(F32)
    for o in (0, 1, 3, 2):
        acc = deliver(sb.take_other(o), acc)

    field = acc + jnp.where(iota((32, 128), 1) < 64, fs[0], fs[1])
    d0, d1 = doubled(field.astype(BF16).astype(F32))
    fs[0] = d0
    fs[1] = d1
    arrive(backin, o_recv.at[1])

    def out_group(g, carry):
        lhs = spread(group_rows(fs, g), 8).astype(BF16)
        acc = nn(lhs, bases[pl.ds(8 * g, 8)].reshape(512, 256))
        for v in range(2):
            here = pl.ds(8 * g, 8)
            out[v, here, :] = acc[8 * v : 8 * v + 8] + nearp[v, here, :] + backin[v, here, :]
        return carry

    lax.fori_loop(0, 4, out_group, 0)
    for copy in pending:
        copy.wait_send()


def shards(
    vectors, self_blocks, near_blocks, near_row, near_col, bases, transfers, far_row, far_col, couplings,
    root_couplings,
):
    vmem = pl.BlockSpec(memory_space=pltpu.VMEM)
    hbm = pl.BlockSpec(memory_space=pl.ANY)
    result = pl.pallas_call(
        kernel,
        out_shape=jax.ShapeDtypeStruct((2, 32, 256), F32),
        in_specs=[hbm] * 11,
        out_specs=vmem,
        scratch_shapes=[
            pltpu.VMEM((32, 2, 256), BF16),
            pltpu.VMEM((1, 32), jnp.int32),
            pltpu.VMEM((1, 32), jnp.int32),
            pltpu.VMEM((1, 128), jnp.int32),
            pltpu.VMEM((1, 128), jnp.int32),
            pltpu.VMEM((32, 256, 256), BF16),
            pltpu.VMEM((32, 256, 256), BF16),
            pltpu.VMEM((32, 64, 256), BF16),
            pltpu.VMEM((62, 64, 64), F32),
            pltpu.VMEM((64, 64, 128), F32),
            pltpu.VMEM((64, 64, 128), F32),
            pltpu.VMEM((2, 32, 256), F32),
            pltpu.VMEM((2, 32, 256), BF16),
            pltpu.VMEM((2, 32, 256), BF16),
            pltpu.VMEM((32, 128), F32),
            pltpu.VMEM((32, 128), F32),
            pltpu.VMEM((2, 32, 128), F32),
            pltpu.VMEM((128, 128), F32),
            pltpu.VMEM((128, 128), F32),
            pltpu.VMEM((2, 32, 256), F32),
            pltpu.VMEM((2, 32, 256), F32),
            pltpu.VMEM((2, 32, 256), F32),
            pltpu.VMEM((2, 32, 256), F32),
            pltpu.VMEM((2, 4, 4, 4, 32, 128), BF16),
            pltpu.VMEM((2, 4, 4, 4, 32, 128), BF16),
            pltpu.VMEM((2, 4, 4, 16, 128), BF16),
            pltpu.VMEM((4, 16, 128), BF16),
            pltpu.VMEM((6, 32, 128), BF16),
            pltpu.VMEM((6, 32, 128), BF16),
            pltpu.SemaphoreType.DMA((11,)),
            pltpu.SemaphoreType.DMA((104,)),
            pltpu.SemaphoreType.DMA((36,)),
            pltpu.SemaphoreType.DMA((36,)),
            pltpu.SemaphoreType.DMA((20,)),
            pltpu.SemaphoreType.DMA((8,)),
        ],
        compiler_params=pltpu.CompilerParams(
            collective_id=0, has_side_effects=True, vmem_limit_bytes=62 * 1024 * 1024
        ),
    )(
        vectors, near_row.reshape(1, 32), near_col.reshape(1, 32), far_row.reshape(1, 128), far_col.reshape(1, 128),
        self_blocks, near_blocks, bases.transpose(0, 2, 1), transfers, couplings.transpose(1, 2, 0),
        root_couplings[0].transpose(1, 2, 0),
    )
    return result.transpose(1, 0, 2)


def solution(mesh):
    both = ("sub", "lvl")
    in_specs = (
        P(both, None, None), P(both, None, None), P(both, None, None), P(both), P(both), P(both, None, None),
        P(both, None, None), P(both), P(both), P(both, None, None), P(both, None, None, None),
    )
    return jax.shard_map(shards, mesh=mesh, in_specs=in_specs, out_specs=P(both, None, None), check_vma=False)
```

```python
import jax
import jax.numpy as jnp
from jax import lax
from jax.experimental import pallas as pl
from jax.experimental.pallas import tpu as pltpu
from jax.sharding import PartitionSpec as P

F32 = jnp.float32
BF16 = jnp.bfloat16
MESH = pl.DeviceIdType.MESH
OFFSETS = (-3, -2, -1, 1, 2, 3)
LEVELS = ((0, 32), (32, 16), (48, 8), (56, 4), (60, 2))


def dot(a, b, ca, cb):
    return lax.dot_general(a, b, (((ca,), (cb,)), ((), ())), preferred_element_type=F32)


def nn(a, b):
    return dot(a, b, 1, 0)


def nt(a, b):
    return dot(a, b, 1, 1)


def tn(a, b):
    return dot(a, b, 0, 0)


def split(x):
    hi = x.astype(BF16)
    return hi, (x - hi.astype(F32)).astype(BF16)


def pick(one_hot, x):
    hi, lo = split(x)
    return nn(one_hot, hi) + nn(one_hot, lo)


def iota(shape, dim):
    return lax.broadcasted_iota(jnp.int32, shape, dim)


def doubled(flat):
    turned = pltpu.roll(flat, 64, 1)
    low = iota(flat.shape, 1) < 64
    return jnp.where(low, flat, turned), jnp.where(low, turned, flat)


def spread(rows, blocks):
    row = iota((16, 128), 0) % 8
    half = iota((16, 128), 1) // 64
    return jnp.concatenate(
        [jnp.where(row == 2 * t + half, rows, 0.0) for t in range(blocks // 2)], axis=1
    )


def collect(wide, blocks):
    row = iota((16, 128), 0) % 8
    half = iota((16, 128), 1) // 64
    total = jnp.zeros((16, 128), F32)
    for t in range(blocks // 2):
        total = total + jnp.where(row == 2 * t + half, wide[:, 128 * t : 128 * t + 128], 0.0)
    return total + pltpu.roll(total, 64, 1)


def joined(rows):
    return jnp.concatenate([rows[0:8, 0:64], rows[8:16, 0:64]], axis=1)


def abreast(rows):
    return jnp.where(iota((8, 128), 1) < 64, rows[0:8], rows[8:16])


def contract(mats, terms, dst):
    t = terms[...]

    def body(i, carry):
        for j in range(8):
            m = mats[8 * i + j]
            for v in range(2):
                row = jnp.sum(m * t[64 * v : 64 * v + 64], axis=0, keepdims=True)
                dst[pl.ds(64 * v + 8 * i + j, 1), :] = row
        return carry

    lax.fori_loop(0, 8, body, 0)


def contract_turned(mats, terms, dst):
    def body(i, carry):
        acc0, acc1 = carry
        for j in range(8):
            m = mats[8 * i + j]
            acc0 = acc0 + m * terms[pl.ds(8 * i + j, 1), :]
            acc1 = acc1 + m * terms[pl.ds(64 + 8 * i + j, 1), :]
        return acc0, acc1

    zero = jnp.zeros((64, 128), F32)
    acc0, acc1 = lax.fori_loop(0, 8, body, (zero, zero))
    dst[0:64, :] = acc0
    dst[64:128, :] = acc1


def tree_up(cs, ps, trans):
    for offset, width in LEVELS:
        count = min(width, 8)
        for g in range(width // count):
            d0, d1 = doubled(cs[8 * g : 8 * g + 8, :])
            lh, ll = split(spread(jnp.concatenate([d0, d1], axis=0), count))
            e = trans[offset + 8 * g : offset + 8 * g + count].reshape(64 * count, 64)
            eh, el = split(e)
            ps[8 * g : 8 * g + 8, :] = joined(nn(lh, eh) + nn(ll, eh) + nn(lh, el))
        half = width // 2
        cs[0:half, :] = ps[pl.ds(0, half, stride=2), :] + ps[pl.ds(1, half, stride=2), :]


def tree_down(fs, trans):
    for offset, width in reversed(LEVELS):
        count = min(width, 8)
        groups = []
        for g in range(width // count):
            f = jnp.concatenate([fs[0, 8 * g : 8 * g + 8, :], fs[1, 8 * g : 8 * g + 8, :]], axis=0)
            fh, fl = split(f[:, 0:64])
            e = trans[offset + 8 * g : offset + 8 * g + count].reshape(64 * count, 64)
            eh, el = split(e)
            groups.append(collect(nt(fh, eh) + nt(fl, eh) + nt(fh, el), count))
        for g, child in enumerate(groups):
            for v in range(2):
                if offset == 0:
                    fs[v, 8 * g : 8 * g + 8, :] = child[8 * v : 8 * v + 8]
                else:
                    fs[v, pl.ds(16 * g, 8, stride=2), :] = child[8 * v : 8 * v + 8]
                    fs[v, pl.ds(16 * g + 1, 8, stride=2), :] = child[8 * v : 8 * v + 8]


def kernel(
    vec_h, near_row_h, near_col_h, far_row_h, far_col_h,
    self_h, near_h, base_h, trans_h, coup_h, root_h,
    out,
    vec, near_row, near_col, far_row, far_col,
    selfs, nears, bases, trans, coup, roots,
    x32, xs, xn, cs, ps, fs, terms, sums, nearp, nwork, back, backin,
    ga, gb, gc, gcin, nsend, nrecv, cnear, picked, partners, outgoing, incoming, halves, other,
    load_sem, send_sem, a_recv, b_recv, c_recv, o_recv, seen, known,
):
    s = lax.axis_index("sub")
    y = lax.axis_index("lvl")
    z = lax.div(s, 8)
    x = lax.rem(lax.div(s, 2), 4)
    c = lax.rem(s, 2)
    me = s * 4 + y

    loads = []
    for i, (src, dst) in enumerate(
        (
            (vec_h, vec), (far_row_h, far_row), (far_col_h, far_col), (near_row_h, near_row), (near_col_h, near_col),
            (base_h, bases), (coup_h, coup), (trans_h, trans), (self_h, selfs), (near_h, nears), (root_h, roots),
        )
    ):
        load = pltpu.make_async_copy(src, dst, load_sem.at[i])
        load.start()
        loads.append(load)

    def at(x=0, y=0, z=0):
        ox, oy, oz = x, y, z
        return (
            (lax.rem(place["z"] + oz, 4) * 4 + lax.rem(place["x"] + ox, 4)) * 2 + c,
            lax.rem(place["y"] + oy, 4),
        )

    place = {"x": x, "y": y, "z": z}
    sibling = ((z * 4 + x) * 2 + 1 - c, y)

    def shifted(o):
        m = lax.rem(me + o + 128, 128)
        return lax.div(m, 4), lax.rem(m, 4)

    barrier = pltpu.get_barrier_semaphore()
    peers = [at(**{d: o}) for d in "xyz" for o in (1, 2, 3)] + [sibling]
    for peer in peers:
        pl.semaphore_signal(barrier, inc=1, device_id=peer, device_id_type=MESH)

    pending = []

    def send(src, dst, rsem, peer):
        copy = pltpu.make_async_remote_copy(
            src_ref=src, dst_ref=dst, send_sem=send_sem.at[len(pending)], recv_sem=rsem,
            device_id=peer, device_id_type=MESH,
        )
        copy.start()
        pending.append(copy)

    def arrive(dst, rsem):
        pltpu.make_async_remote_copy(
            src_ref=dst, dst_ref=dst, send_sem=send_sem.at[0], recv_sem=rsem,
            device_id=sibling, device_id_type=MESH,
        ).wait_recv()

    def back_by(index, o):
        return lax.rem(index + 4 - o, 4)

    for i in range(5):
        loads[i].wait()
    for v in range(2):
        xv = vec[:, v, :].astype(F32)
        x32[v, 0:32, :] = xv
        xs[v] = xv.astype(BF16)

    row16 = iota((16, 256), 0) % 8
    far_r = far_row[...]
    far_c = far_col[...]
    own_hot = (iota((32, 128), 0) == far_r).astype(BF16)

    def group_rows(ref, g):
        return jnp.concatenate([ref[0, pl.ds(8 * g, 8), :], ref[1, pl.ds(8 * g, 8), :]], axis=0)

    loads[5].wait()

    def coeff_group(g, carry):
        wide = nt(group_rows(x32, g).astype(BF16), bases[pl.ds(8 * g, 8)].reshape(512, 256))
        cs[pl.ds(8 * g, 8), :] = abreast(collect(wide, 8))
        return carry

    lax.fori_loop(0, 4, coeff_group, 0)
    ch, cl = split(cs[...])
    ga[x, z, c] = ch

    terms[...] = tn(ch, own_hot) + tn(cl, own_hot)
    loads[6].wait()
    contract_turned(coup, terms, sums)
    bh, bl = split(sums[...])
    dev = far_c // 32
    dist = (dev - me + 128) % 128
    is_far = (dist > 3) & (dist < 125)
    before = (iota((128, 128), 0) < iota((128, 128), 1)).astype(BF16)
    pos = nn(jnp.broadcast_to(is_far.astype(F32), (16, 128)).astype(BF16), before)[0:1, :].astype(jnp.int32)
    pos = jnp.where(is_far, pos, -1000)
    far_hot = (iota((32, 128), 0) == pos).astype(BF16)
    gb[x, y] = nt(far_hot, bh).astype(BF16)
    leaf_of = iota((32, 128), 0)
    near_hot = jnp.concatenate(
        [(leaf_of + ((me + o + 128) % 128) * 32 == far_c).astype(BF16) for o in OFFSETS], axis=0
    )
    nsend[...] = (nt(near_hot, bh) + nt(near_hot, bl)).astype(BF16).reshape(6, 32, 128)

    loads[7].wait()
    tree_up(cs, ps, trans)
    rh, rl = split(cs[0:1, :])
    lane_hot = (iota((128, 128), 0) == pos + 32 * y).astype(BF16)
    row_id = iota((16, 128), 0)
    codes = jnp.where(row_id == 0, dev, jnp.where(row_id == 1, far_c - dev * 32, 0)).astype(F32).astype(BF16)
    tile = nt(codes, lane_hot)
    tile = jnp.where(row_id == 4 + 2 * y, rh.astype(F32), tile)
    tile = jnp.where(row_id == 5 + 2 * y, rl.astype(F32), tile)
    gcin[y] = tile.astype(BF16)

    pl.semaphore_wait(barrier, len(peers))
    for o in (1, 2, 3):
        pl.semaphore_signal(seen, inc=1, device_id=at(x=o), device_id_type=MESH)
    send(ga.at[x, z, c], ga.at[x, z, c], a_recv.at[0], sibling)
    for o in (2, 1, 3):
        send(gcin.at[y], gcin.at[y], c_recv.at[o], at(y=o))
        send(gb.at[x, y], gb.at[x, y], b_recv.at[o], at(y=o))

    def run_blocks(src, dst, blocks, product):
        def body(g, carry):
            rows = group_rows(src, g)
            acc = jnp.zeros((16, 256), F32)
            for j in range(8):
                acc = acc + product(jnp.where(row16 == j, rows, 0.0).astype(BF16), blocks[8 * g + j])
            for v in range(2):
                dst[v, pl.ds(8 * g, 8), :] = acc[8 * v : 8 * v + 8]
            return carry

        lax.fori_loop(0, 4, body, 0)

    arrive(ga.at[x, z, 1 - c], a_recv.at[0])
    for o in (2, 1, 3):
        send(ga.at[x, z], ga.at[x, z], a_recv.at[o], at(z=o))
    loads[8].wait()
    run_blocks(x32, nearp, selfs, nt)

    row_hot = (iota((32, 32), 0) == near_row[...]).astype(BF16)
    col_hot = (iota((64, 32), 0) == near_col[...]).astype(BF16)
    for v in range(2):
        nwork[v] = tn(row_hot, xs[v])
    loads[9].wait()
    run_blocks(nwork, nwork, nears, nn)

    for o in (1, 3, 2):
        arrive(gcin.at[back_by(y, o)], c_recv.at[o])
    pl.semaphore_wait(seen, 3)
    merged = gcin[0].astype(F32) + gcin[1].astype(F32) + gcin[2].astype(F32) + gcin[3].astype(F32)
    gc[c, z, x] = merged.astype(BF16)
    beside = [at(x=1), at(x=3), at(x=1, z=1), at(x=3, z=3)]
    for peer in beside:
        pl.semaphore_signal(known, inc=1, device_id=peer, device_id_type=MESH)
    for i, j in ((0, 2), (0, 1), (0, 3), (2, 2), (2, 1), (2, 3), (1, 2), (3, 2), (1, 1), (1, 3), (3, 1), (3, 3), (2, 0), (1, 0), (3, 0)):
        k = 4 + 4 * i + (j if i == 0 else 0)
        send(gc.at[c, z, x], gc.at[c, z, x], c_recv.at[k], at(z=i, x=j))
    for o in (1, 3, 2):
        arrive(gb.at[x, back_by(y, o)], b_recv.at[o])
    for o in (2, 1, 3):
        send(gb.at[x], gb.at[x], b_recv.at[3 + o], at(x=o))

    def decode(t):
        d = t[0:1, :].astype(jnp.int32)
        return d % 4, d // 32, (d // 8) % 4, (d // 4) % 2, t[1:2, :].astype(jnp.int32)

    ty, tz, tx, tc, tleaf = decode(merged)
    slot = jnp.where(ty == y, ((tx * 4 + tz) * 2 + tc) * 32 + tleaf, -1).astype(F32)
    slots = jnp.transpose(jnp.broadcast_to(slot, (128, 128)))
    slot_hot = jnp.concatenate(
        [(slots == (iota((128, 128), 1) + 128 * i).astype(F32)).astype(BF16) for i in range(8)], axis=1
    )

    for v in range(2):
        both = pick(col_hot, nwork[v])
        nearp[v] = nearp[v] + both[0:32]
        back[v] = both[32:64]

    for o in (1, 3, 2):
        arrive(ga.at[x, back_by(z, o)], a_recv.at[o])
    for o in (2, 1, 3):
        send(ga.at[x], ga.at[x], a_recv.at[3 + o], at(x=o))

    pl.semaphore_wait(known, len(beside))
    send(xs, xn, o_recv.at[0], shifted(-1))
    for i, o in enumerate(OFFSETS):
        send(ga.at[x, z, c], cnear.at[5 - i], o_recv.at[13 - i], shifted(o))
    for i, o in enumerate(OFFSETS):
        send(nsend.at[i], nrecv.at[i], o_recv.at[2 + i], shifted(o))
    send(back, backin, o_recv.at[1], shifted(1))

    for j in (1, 3, 2):
        arrive(gc.at[c, z, back_by(x, j)], c_recv.at[4 + j])
        arrive(gb.at[back_by(x, j)], b_recv.at[3 + j])
    hots = []
    for j in range(4):
        ty, tz, tx, tc, tleaf = decode(gc[c, z, j].astype(F32))
        line = jnp.where((ty == y) & (tx == x), (tz * 2 + tc) * 32 + tleaf, -1)
        hots.append((iota((256, 128), 0) == line).astype(F32).astype(BF16))
    outgoing[...] = nn(jnp.concatenate(hots, axis=1), gb[...].reshape(512, 128)).reshape(4, 64, 128)
    for o in (2, 1, 3):
        to = lax.rem(z + o, 4)
        send(outgoing.at[to], incoming.at[z], b_recv.at[6 + o], at(z=o))
    incoming[z] = outgoing[z]

    for o in (1, 3, 2):
        arrive(ga.at[back_by(x, o)], a_recv.at[3 + o])
    picked[...] = nn(slot_hot, ga[...].reshape(1024, 128)).astype(BF16).reshape(4, 32, 128)
    for o in (2, 1, 3):
        to = lax.rem(y + o, 4)
        send(picked.at[to], partners.at[y], a_recv.at[6 + o], at(y=o))
    partners[y] = picked[y]

    for i in (1, 3, 2):
        arrive(gc.at[c, back_by(z, i)], c_recv.at[4 + 4 * i])
    send(gc.at[c], gc.at[c], c_recv.at[0], sibling)

    arrive(xn, o_recv.at[0])
    for v in range(2):
        nwork[v] = tn(col_hot, jnp.concatenate([xs[v], xn[v]], axis=0))
    run_blocks(nwork, nwork, nears, nt)
    for v in range(2):
        nearp[v] = nearp[v] + pick(row_hot, nwork[v])

    arrive(gc.at[1 - c], c_recv.at[0])
    row_at = iota((128, 512), 1)
    tile_at = row_at // 16
    line = row_at % 16
    holder = (((tile_at // 4) % 4 * 4 + tile_at % 4) * 2 + tile_at // 16) * 4 + (line - 4) // 2
    sel = ((holder == iota((128, 512), 0)) & (line >= 4) & (line < 12)).astype(BF16)
    terms[...] = jnp.transpose(nn(sel, gc[...].reshape(512, 128)))
    loads[10].wait()
    contract(roots, terms, sums)
    sh, sl = split(sums[...])
    ones = jnp.ones((16, 128), BF16)
    top = (nt(ones, sh) + nt(ones, sl))[0:8]
    d0, d1 = doubled(top)
    fs[0, 0:8, :] = d0
    fs[1, 0:8, :] = d1
    tree_down(fs, trans)

    for o in (1, 3, 2):
        arrive(incoming.at[back_by(z, o)], b_recv.at[6 + o])
    total = incoming[0] + incoming[1] + incoming[2] + incoming[3]
    halves[0] = total[0:32]
    halves[1] = total[32:64]
    send(halves.at[1 - c], other, b_recv.at[0], sibling)
    for i in range(6):
        arrive(cnear.at[i], o_recv.at[8 + i])
    near_terms = tn(cnear[...].reshape(192, 128), near_hot)
    acc = halves[c]
    for i in range(6):
        arrive(nrecv.at[i], o_recv.at[2 + i])
        acc = acc + nrecv[i].astype(F32)
    for o in (1, 3, 2):
        arrive(partners.at[back_by(y, o)], a_recv.at[6 + o])
    rows = partners[0].astype(F32) + partners[1].astype(F32) + partners[2].astype(F32) + partners[3].astype(F32)
    terms[...] = near_terms + tn(rows.astype(BF16), far_hot)
    contract(coup, terms, sums)
    sh, sl = split(sums[...])
    acc = acc + nt(own_hot, sh) + nt(own_hot, sl)
    arrive(other, b_recv.at[0])
    acc = acc + other[...]

    field = acc + jnp.where(iota((32, 128), 1) < 64, fs[0], fs[1])
    d0, d1 = doubled(field.astype(BF16).astype(F32))
    fs[0] = d0
    fs[1] = d1
    arrive(backin, o_recv.at[1])

    def out_group(g, carry):
        lhs = spread(group_rows(fs, g), 8).astype(BF16)
        acc = nn(lhs, bases[pl.ds(8 * g, 8)].reshape(512, 256))
        for v in range(2):
            here = pl.ds(8 * g, 8)
            out[v, here, :] = acc[8 * v : 8 * v + 8] + nearp[v, here, :] + backin[v, here, :]
        return carry

    lax.fori_loop(0, 4, out_group, 0)
    for copy in pending:
        copy.wait_send()


def shards(
    vectors, self_blocks, near_blocks, near_row, near_col, bases, transfers, far_row, far_col, couplings,
    root_couplings,
):
    vmem = pl.BlockSpec(memory_space=pltpu.VMEM)
    hbm = pl.BlockSpec(memory_space=pl.ANY)
    result = pl.pallas_call(
        kernel,
        out_shape=jax.ShapeDtypeStruct((2, 32, 256), F32),
        in_specs=[hbm] * 11,
        out_specs=vmem,
        scratch_shapes=[
            pltpu.VMEM((32, 2, 256), BF16),
            pltpu.VMEM((1, 32), jnp.int32),
            pltpu.VMEM((1, 32), jnp.int32),
            pltpu.VMEM((1, 128), jnp.int32),
            pltpu.VMEM((1, 128), jnp.int32),
            pltpu.VMEM((32, 256, 256), BF16),
            pltpu.VMEM((32, 256, 256), BF16),
            pltpu.VMEM((32, 64, 256), BF16),
            pltpu.VMEM((62, 64, 64), F32),
            pltpu.VMEM((64, 64, 128), F32),
            pltpu.VMEM((64, 64, 128), F32),
            pltpu.VMEM((2, 32, 256), F32),
            pltpu.VMEM((2, 32, 256), BF16),
            pltpu.VMEM((2, 32, 256), BF16),
            pltpu.VMEM((32, 128), F32),
            pltpu.VMEM((32, 128), F32),
            pltpu.VMEM((2, 32, 128), F32),
            pltpu.VMEM((128, 128), F32),
            pltpu.VMEM((128, 128), F32),
            pltpu.VMEM((2, 32, 256), F32),
            pltpu.VMEM((2, 32, 256), F32),
            pltpu.VMEM((2, 32, 256), F32),
            pltpu.VMEM((2, 32, 256), F32),
            pltpu.VMEM((4, 4, 2, 32, 128), BF16),
            pltpu.VMEM((4, 4, 32, 128), BF16),
            pltpu.VMEM((2, 4, 4, 16, 128), BF16),
            pltpu.VMEM((4, 16, 128), BF16),
            pltpu.VMEM((6, 32, 128), BF16),
            pltpu.VMEM((6, 32, 128), BF16),
            pltpu.VMEM((6, 32, 128), BF16),
            pltpu.VMEM((4, 32, 128), BF16),
            pltpu.VMEM((4, 32, 128), BF16),
            pltpu.VMEM((4, 64, 128), F32),
            pltpu.VMEM((4, 64, 128), F32),
            pltpu.VMEM((2, 32, 128), F32),
            pltpu.VMEM((32, 128), F32),
            pltpu.SemaphoreType.DMA((11,)),
            pltpu.SemaphoreType.DMA((104,)),
            pltpu.SemaphoreType.DMA((10,)),
            pltpu.SemaphoreType.DMA((10,)),
            pltpu.SemaphoreType.DMA((20,)),
            pltpu.SemaphoreType.DMA((14,)),
            pltpu.SemaphoreType.REGULAR,
            pltpu.SemaphoreType.REGULAR,
        ],
        compiler_params=pltpu.CompilerParams(
            collective_id=0, has_side_effects=True, vmem_limit_bytes=62 * 1024 * 1024
        ),
    )(
        vectors, near_row.reshape(1, 32), near_col.reshape(1, 32), far_row.reshape(1, 128), far_col.reshape(1, 128),
        self_blocks, near_blocks, bases.transpose(0, 2, 1), transfers, couplings.transpose(1, 2, 0),
        root_couplings[0].transpose(1, 2, 0),
    )
    return result.transpose(1, 0, 2)


def solution(mesh):
    both = ("sub", "lvl")
    in_specs = (
        P(both, None, None), P(both, None, None), P(both, None, None), P(both), P(both), P(both, None, None),
        P(both, None, None), P(both), P(both), P(both, None, None), P(both, None, None, None),
    )
    return jax.shard_map(shards, mesh=mesh, in_specs=in_specs, out_specs=P(both, None, None), check_vma=False)
```

```python
import jax
import jax.numpy as jnp
from jax import lax
from jax.experimental import pallas as pl
from jax.experimental.pallas import tpu as pltpu
from jax.sharding import PartitionSpec as P

F32 = jnp.float32
BF16 = jnp.bfloat16
MESH = pl.DeviceIdType.MESH
OFFSETS = (-3, -2, -1, 1, 2, 3)
LEVELS = ((0, 32), (32, 16), (48, 8), (56, 4), (60, 2))


def dot(a, b, ca, cb):
    return lax.dot_general(a, b, (((ca,), (cb,)), ((), ())), preferred_element_type=F32)


def nn(a, b):
    return dot(a, b, 1, 0)


def nt(a, b):
    return dot(a, b, 1, 1)


def tn(a, b):
    return dot(a, b, 0, 0)


def split(x):
    hi = x.astype(BF16)
    return hi, (x - hi.astype(F32)).astype(BF16)


def pick(one_hot, x):
    hi, lo = split(x)
    return nn(one_hot, hi) + nn(one_hot, lo)


def iota(shape, dim):
    return lax.broadcasted_iota(jnp.int32, shape, dim)


def doubled(flat):
    turned = pltpu.roll(flat, 64, 1)
    low = iota(flat.shape, 1) < 64
    return jnp.where(low, flat, turned), jnp.where(low, turned, flat)


def spread(rows, blocks):
    row = iota((16, 128), 0) % 8
    half = iota((16, 128), 1) // 64
    return jnp.concatenate(
        [jnp.where(row == 2 * t + half, rows, 0.0) for t in range(blocks // 2)], axis=1
    )


def collect(wide, blocks):
    row = iota((16, 128), 0) % 8
    half = iota((16, 128), 1) // 64
    total = jnp.zeros((16, 128), F32)
    for t in range(blocks // 2):
        total = total + jnp.where(row == 2 * t + half, wide[:, 128 * t : 128 * t + 128], 0.0)
    return total + pltpu.roll(total, 64, 1)


def joined(rows):
    return jnp.concatenate([rows[0:8, 0:64], rows[8:16, 0:64]], axis=1)


def abreast(rows):
    return jnp.where(iota((8, 128), 1) < 64, rows[0:8], rows[8:16])


def contract(mats, terms, dst):
    t = terms[...]

    def body(i, carry):
        for j in range(8):
            m = mats[8 * i + j]
            for v in range(2):
                row = jnp.sum(m * t[64 * v : 64 * v + 64], axis=0, keepdims=True)
                dst[pl.ds(64 * v + 8 * i + j, 1), :] = row
        return carry

    lax.fori_loop(0, 8, body, 0)


def contract_turned(mats, terms, dst):
    def body(i, carry):
        acc0, acc1 = carry
        for j in range(8):
            m = mats[8 * i + j]
            acc0 = acc0 + m * terms[pl.ds(8 * i + j, 1), :]
            acc1 = acc1 + m * terms[pl.ds(64 + 8 * i + j, 1), :]
        return acc0, acc1

    zero = jnp.zeros((64, 128), F32)
    acc0, acc1 = lax.fori_loop(0, 8, body, (zero, zero))
    dst[0:64, :] = acc0
    dst[64:128, :] = acc1


def tree_up(cs, ps, trans):
    for offset, width in LEVELS:
        count = min(width, 8)
        for g in range(width // count):
            d0, d1 = doubled(cs[8 * g : 8 * g + 8, :])
            lh, ll = split(spread(jnp.concatenate([d0, d1], axis=0), count))
            e = trans[offset + 8 * g : offset + 8 * g + count].reshape(64 * count, 64)
            eh, el = split(e)
            ps[8 * g : 8 * g + 8, :] = joined(nn(lh, eh) + nn(ll, eh) + nn(lh, el))
        half = width // 2
        cs[0:half, :] = ps[pl.ds(0, half, stride=2), :] + ps[pl.ds(1, half, stride=2), :]


def tree_down(fs, halved):
    for offset, width in reversed(LEVELS):
        count = min(width, 8)
        groups = []
        for g in range(width // count):
            f = jnp.concatenate([fs[0, 8 * g : 8 * g + 8, :], fs[1, 8 * g : 8 * g + 8, :]], axis=0)
            fh, fl = split(f[:, 0:64])
            here = slice(offset + 8 * g, offset + 8 * g + count)
            eh = halved[0, here].reshape(64 * count, 64)
            el = halved[1, here].reshape(64 * count, 64)
            main = nt(jnp.concatenate([fh, fl], axis=0), eh)
            groups.append(collect(main[0:16] + main[16:32] + nt(fh, el), count))
        for g, child in enumerate(groups):
            for v in range(2):
                if offset == 0:
                    fs[v, 8 * g : 8 * g + 8, :] = child[8 * v : 8 * v + 8]
                else:
                    fs[v, pl.ds(16 * g, 8, stride=2), :] = child[8 * v : 8 * v + 8]
                    fs[v, pl.ds(16 * g + 1, 8, stride=2), :] = child[8 * v : 8 * v + 8]


def kernel(
    vec_h, near_row_h, near_col_h, far_row_h, far_col_h,
    self_h, near_h, base_h, trans_h, coup_h, root_h,
    out,
    vec, near_row, near_col, far_row, far_col,
    selfs, nears, bases, trans, coup, roots,
    halved, x32, xs, xn, cs, ps, fs, terms, sums, nearp, nwork, back, backin,
    ga, gb, gc, gcin, gq, gqin, nsend, nrecv, cnear, picked, partners, outgoing, incoming, halves, other,
    load_sem, send_sem, a_recv, b_recv, c_recv, o_recv, seen, known,
):
    s = lax.axis_index("sub")
    y = lax.axis_index("lvl")
    z = lax.div(s, 8)
    x = lax.rem(lax.div(s, 2), 4)
    c = lax.rem(s, 2)
    me = s * 4 + y

    loads = []
    for i, (src, dst) in enumerate(
        (
            (vec_h, vec), (far_row_h, far_row), (far_col_h, far_col), (near_row_h, near_row), (near_col_h, near_col),
            (base_h, bases), (coup_h, coup), (trans_h, trans), (self_h, selfs), (near_h, nears), (root_h, roots),
        )
    ):
        load = pltpu.make_async_copy(src, dst, load_sem.at[i])
        load.start()
        loads.append(load)

    def at(x=0, y=0, z=0):
        ox, oy, oz = x, y, z
        return (
            (lax.rem(place["z"] + oz, 4) * 4 + lax.rem(place["x"] + ox, 4)) * 2 + c,
            lax.rem(place["y"] + oy, 4),
        )

    place = {"x": x, "y": y, "z": z}
    sibling = ((z * 4 + x) * 2 + 1 - c, y)

    def shifted(o):
        m = lax.rem(me + o + 128, 128)
        return lax.div(m, 4), lax.rem(m, 4)

    barrier = pltpu.get_barrier_semaphore()
    peers = [at(**{d: o}) for d in "xyz" for o in (1, 2, 3)] + [sibling]
    for peer in peers:
        pl.semaphore_signal(barrier, inc=1, device_id=peer, device_id_type=MESH)

    pending = []

    def send(src, dst, rsem, peer):
        copy = pltpu.make_async_remote_copy(
            src_ref=src, dst_ref=dst, send_sem=send_sem.at[len(pending)], recv_sem=rsem,
            device_id=peer, device_id_type=MESH,
        )
        copy.start()
        pending.append(copy)

    def arrive(dst, rsem):
        pltpu.make_async_remote_copy(
            src_ref=dst, dst_ref=dst, send_sem=send_sem.at[0], recv_sem=rsem,
            device_id=sibling, device_id_type=MESH,
        ).wait_recv()

    def back_by(index, o):
        return lax.rem(index + 4 - o, 4)

    for i in range(5):
        loads[i].wait()
    for v in range(2):
        xv = vec[:, v, :].astype(F32)
        x32[v, 0:32, :] = xv
        xs[v] = xv.astype(BF16)

    row16 = iota((16, 256), 0) % 8
    far_r = far_row[...]
    far_c = far_col[...]
    own_hot = (iota((32, 128), 0) == far_r).astype(BF16)

    def group_rows(ref, g):
        return jnp.concatenate([ref[0, pl.ds(8 * g, 8), :], ref[1, pl.ds(8 * g, 8), :]], axis=0)

    loads[5].wait()

    def coeff_group(g, carry):
        wide = nt(group_rows(x32, g).astype(BF16), bases[pl.ds(8 * g, 8)].reshape(512, 256))
        cs[pl.ds(8 * g, 8), :] = abreast(collect(wide, 8))
        return carry

    lax.fori_loop(0, 4, coeff_group, 0)
    ch, cl = split(cs[...])
    ga[z, x, c] = ch

    terms[...] = tn(ch, own_hot) + tn(cl, own_hot)
    loads[6].wait()
    contract_turned(coup, terms, sums)
    bh, bl = split(sums[...])
    dev = far_c // 32
    dist = (dev - me + 128) % 128
    is_far = (dist > 3) & (dist < 125)
    before = (iota((128, 128), 0) < iota((128, 128), 1)).astype(BF16)
    pos = nn(jnp.broadcast_to(is_far.astype(F32), (16, 128)).astype(BF16), before)[0:1, :].astype(jnp.int32)
    pos = jnp.where(is_far, pos, -1000)
    far_hot = (iota((32, 128), 0) == pos).astype(BF16)
    gb[x, y] = nt(far_hot, bh).astype(BF16)
    lane_hot = (iota((128, 128), 0) == pos + 32 * y).astype(BF16)
    row_id = iota((16, 128), 0)
    codes = jnp.where(row_id == 0, dev, jnp.where(row_id == 1, far_c - dev * 32, 0)).astype(F32).astype(BF16)
    gqin[y] = nt(codes, lane_hot).astype(BF16)
    pl.semaphore_wait(barrier, len(peers))
    send(ga.at[z, x, c], ga.at[z, x, c], a_recv.at[0], sibling)
    for o in (1, 2, 3):
        pl.semaphore_signal(seen, inc=1, device_id=at(x=o), device_id_type=MESH)
        pl.semaphore_signal(seen, inc=1, device_id=at(y=o), device_id_type=MESH)
    for o in (2, 1, 3):
        send(gqin.at[y], gqin.at[y], c_recv.at[16 + o], at(y=o))
        send(gb.at[x, y], gb.at[x, y], b_recv.at[o], at(y=o))

    arrive(ga.at[z, x, 1 - c], a_recv.at[0])
    for o in (2, 1, 3):
        send(ga.at[z, x], ga.at[z, x], a_recv.at[o], at(x=o))
    for o in (2, 1, 3):
        send(ga.at[z, x], ga.at[z, x], a_recv.at[3 + o], at(z=o))
        send(gb.at[x, y], gb.at[x, y], b_recv.at[3 + o], at(x=o))

    leaf_of = iota((32, 128), 0)
    near_hot = jnp.concatenate(
        [(leaf_of + ((me + o + 128) % 128) * 32 == far_c).astype(BF16) for o in OFFSETS], axis=0
    )
    nsend[...] = (nt(near_hot, bh) + nt(near_hot, bl)).astype(BF16).reshape(6, 32, 128)

    loads[7].wait()
    tree_up(cs, ps, trans)
    rh, rl = split(cs[0:1, :])
    tile = jnp.where(row_id == 4 + 2 * y, rh.astype(F32), jnp.where(row_id == 5 + 2 * y, rl.astype(F32), 0.0))
    gcin[y] = tile.astype(BF16)
    for o in (2, 1, 3):
        send(gcin.at[y], gcin.at[y], c_recv.at[o], at(y=o))

    pl.semaphore_wait(seen, 6)
    beside = [at(x=1), at(x=3), at(x=1, z=1), at(x=3, z=3)]
    for peer in beside:
        pl.semaphore_signal(known, inc=1, device_id=peer, device_id_type=MESH)

    def run_blocks(src, dst, blocks, product):
        def body(g, carry):
            rows = group_rows(src, g)
            acc = jnp.zeros((16, 256), F32)
            for j in range(8):
                acc = acc + product(jnp.where(row16 == j, rows, 0.0).astype(BF16), blocks[8 * g + j])
            for v in range(2):
                dst[v, pl.ds(8 * g, 8), :] = acc[8 * v : 8 * v + 8]
            return carry

        lax.fori_loop(0, 4, body, 0)

    loads[8].wait()
    run_blocks(x32, nearp, selfs, nt)

    for o in (1, 3, 2):
        block = ga.at[z, back_by(x, o)]
        arrive(block, a_recv.at[o])
        for p in (2, 1, 3):
            send(block, block, a_recv.at[3 + p], at(z=p))
    for o in (1, 3, 2):
        block = gb.at[x, back_by(y, o)]
        arrive(gqin.at[back_by(y, o)], c_recv.at[16 + o])
        arrive(block, b_recv.at[o])
        for p in (2, 1, 3):
            send(block, block, b_recv.at[3 + p], at(x=p))
    merged = gqin[0].astype(F32) + gqin[1].astype(F32) + gqin[2].astype(F32) + gqin[3].astype(F32)
    gq[x] = merged.astype(BF16)
    for o in (2, 1, 3):
        send(gq.at[x], gq.at[x], c_recv.at[19 + o], at(x=o))

    for o in (1, 3, 2):
        arrive(gcin.at[back_by(y, o)], c_recv.at[o])
    gc[c, z, x] = (
        gcin[0].astype(F32) + gcin[1].astype(F32) + gcin[2].astype(F32) + gcin[3].astype(F32)
    ).astype(BF16)
    for i, j in ((2, 2), (2, 1), (2, 3), (1, 2), (3, 2), (1, 1), (1, 3), (3, 1), (3, 3), (0, 2), (2, 0), (0, 1), (0, 3), (1, 0), (3, 0)):
        k = 4 + 4 * i + (j if i == 0 else 0)
        send(gc.at[c, z, x], gc.at[c, z, x], c_recv.at[k], at(z=i, x=j))

    pl.semaphore_wait(known, len(beside))
    send(xs, xn, o_recv.at[0], shifted(-1))
    for i, o in enumerate(OFFSETS):
        send(ga.at[z, x, c], cnear.at[5 - i], o_recv.at[13 - i], shifted(o))
    for i, o in enumerate(OFFSETS):
        send(nsend.at[i], nrecv.at[i], o_recv.at[2 + i], shifted(o))

    row_hot = (iota((32, 32), 0) == near_row[...]).astype(BF16)
    col_hot = (iota((64, 32), 0) == near_col[...]).astype(BF16)
    for v in range(2):
        nwork[v] = tn(row_hot, xs[v])
    loads[9].wait()
    run_blocks(nwork, nwork, nears, nn)

    for v in range(2):
        both = pick(col_hot, nwork[v])
        nearp[v] = nearp[v] + both[0:32]
        back[v] = both[32:64]

    send(back, backin, o_recv.at[1], shifted(1))

    def decode(t):
        d = t[0:1, :].astype(jnp.int32)
        return d % 4, d // 32, (d // 8) % 4, (d // 4) % 2, t[1:2, :].astype(jnp.int32)

    ty, tz, tx, tc, tleaf = decode(merged)
    slot = jnp.where(ty == y, ((tz * 4 + tx) * 2 + tc) * 32 + tleaf, -1).astype(F32)
    slots = jnp.transpose(jnp.broadcast_to(slot, (128, 128)))
    slot_hot = jnp.concatenate(
        [(slots == (iota((128, 128), 1) + 128 * i).astype(F32)).astype(BF16) for i in range(8)], axis=1
    )

    for j in (1, 3, 2):
        arrive(gq.at[back_by(x, j)], c_recv.at[19 + j])
        arrive(gb.at[back_by(x, j)], b_recv.at[3 + j])
    hots = []
    for j in range(4):
        ty, tz, tx, tc, tleaf = decode(gq[j].astype(F32))
        line = jnp.where((ty == y) & (tx == x), (tz * 2 + tc) * 32 + tleaf, -1)
        hots.append((iota((256, 128), 0) == line).astype(F32).astype(BF16))
    outgoing[...] = nn(jnp.concatenate(hots, axis=1), gb[...].reshape(512, 128)).reshape(4, 64, 128)
    for o in (2, 1, 3):
        to = lax.rem(z + o, 4)
        send(outgoing.at[to], incoming.at[z], b_recv.at[6 + o], at(z=o))
    incoming[z] = outgoing[z]

    for o in (1, 3, 2):
        arrive(ga.at[back_by(z, o)], a_recv.at[3 + o])
    picked[...] = nn(slot_hot, ga[...].reshape(1024, 128)).astype(BF16).reshape(4, 32, 128)
    for o in (2, 1, 3):
        to = lax.rem(y + o, 4)
        send(picked.at[to], partners.at[y], a_recv.at[6 + o], at(y=o))
    partners[y] = picked[y]

    def halve(i, carry):
        hi, lo = split(trans[pl.ds(2 * i, 2)])
        halved[0, pl.ds(2 * i, 2)] = hi
        halved[1, pl.ds(2 * i, 2)] = lo
        return carry

    lax.fori_loop(0, 31, halve, 0)
    row_at = iota((128, 512), 1)
    tile_at = row_at // 16
    line = row_at % 16
    holder = (((tile_at // 4) % 4 * 4 + tile_at % 4) * 2 + tile_at // 16) * 4 + (line - 4) // 2
    sel = ((holder == iota((128, 512), 0)) & (line >= 4) & (line < 12)).astype(BF16)
    for j in (1, 3, 2):
        arrive(gc.at[c, z, back_by(x, j)], c_recv.at[4 + j])
    for i in (1, 3, 2):
        arrive(gc.at[c, back_by(z, i)], c_recv.at[4 + 4 * i])
    send(gc.at[c], gc.at[c], c_recv.at[0], sibling)

    arrive(xn, o_recv.at[0])
    for v in range(2):
        nwork[v] = tn(col_hot, jnp.concatenate([xs[v], xn[v]], axis=0))
    run_blocks(nwork, nwork, nears, nt)
    for v in range(2):
        nearp[v] = nearp[v] + pick(row_hot, nwork[v])

    for o in (1, 3, 2):
        arrive(incoming.at[back_by(z, o)], b_recv.at[6 + o])
    total = incoming[0] + incoming[1] + incoming[2] + incoming[3]
    halves[0] = total[0:32]
    halves[1] = total[32:64]
    send(halves.at[1 - c], other, b_recv.at[0], sibling)
    for i in range(6):
        arrive(cnear.at[i], o_recv.at[8 + i])
    near_terms = tn(cnear[...].reshape(192, 128), near_hot)
    acc = halves[c]
    for i in range(6):
        arrive(nrecv.at[i], o_recv.at[2 + i])
        acc = acc + nrecv[i].astype(F32)

    arrive(gc.at[1 - c], c_recv.at[0])
    terms[...] = jnp.transpose(nn(sel, gc[...].reshape(512, 128)))
    loads[10].wait()
    contract(roots, terms, sums)
    sh, sl = split(sums[...])
    ones = jnp.ones((16, 128), BF16)
    top = (nt(ones, sh) + nt(ones, sl))[0:8]
    d0, d1 = doubled(top)
    fs[0, 0:8, :] = d0
    fs[1, 0:8, :] = d1
    tree_down(fs, halved)

    for o in (1, 3, 2):
        arrive(partners.at[back_by(y, o)], a_recv.at[6 + o])
    rows = partners[0].astype(F32) + partners[1].astype(F32) + partners[2].astype(F32) + partners[3].astype(F32)
    terms[...] = near_terms + tn(rows.astype(BF16), far_hot)
    contract(coup, terms, sums)
    sh, sl = split(sums[...])
    acc = acc + nt(own_hot, sh) + nt(own_hot, sl)
    arrive(other, b_recv.at[0])
    acc = acc + other[...]

    field = acc + jnp.where(iota((32, 128), 1) < 64, fs[0], fs[1])
    d0, d1 = doubled(field.astype(BF16).astype(F32))
    fs[0] = d0
    fs[1] = d1
    arrive(backin, o_recv.at[1])

    def out_group(g, carry):
        lhs = spread(group_rows(fs, g), 8).astype(BF16)
        acc = nn(lhs, bases[pl.ds(8 * g, 8)].reshape(512, 256))
        for v in range(2):
            here = pl.ds(8 * g, 8)
            out[v, here, :] = acc[8 * v : 8 * v + 8] + nearp[v, here, :] + backin[v, here, :]
        return carry

    lax.fori_loop(0, 4, out_group, 0)
    for copy in pending:
        copy.wait_send()


def shards(
    vectors, self_blocks, near_blocks, near_row, near_col, bases, transfers, far_row, far_col, couplings,
    root_couplings,
):
    vmem = pl.BlockSpec(memory_space=pltpu.VMEM)
    hbm = pl.BlockSpec(memory_space=pl.ANY)
    result = pl.pallas_call(
        kernel,
        out_shape=jax.ShapeDtypeStruct((2, 32, 256), F32),
        in_specs=[hbm] * 11,
        out_specs=vmem,
        scratch_shapes=[
            pltpu.VMEM((32, 2, 256), BF16),
            pltpu.VMEM((1, 32), jnp.int32),
            pltpu.VMEM((1, 32), jnp.int32),
            pltpu.VMEM((1, 128), jnp.int32),
            pltpu.VMEM((1, 128), jnp.int32),
            pltpu.VMEM((32, 256, 256), BF16),
            pltpu.VMEM((32, 256, 256), BF16),
            pltpu.VMEM((32, 64, 256), BF16),
            pltpu.VMEM((62, 64, 64), F32),
            pltpu.VMEM((64, 64, 128), F32),
            pltpu.VMEM((64, 64, 128), F32),
            pltpu.VMEM((2, 62, 64, 64), BF16),
            pltpu.VMEM((2, 32, 256), F32),
            pltpu.VMEM((2, 32, 256), BF16),
            pltpu.VMEM((2, 32, 256), BF16),
            pltpu.VMEM((32, 128), F32),
            pltpu.VMEM((32, 128), F32),
            pltpu.VMEM((2, 32, 128), F32),
            pltpu.VMEM((128, 128), F32),
            pltpu.VMEM((128, 128), F32),
            pltpu.VMEM((2, 32, 256), F32),
            pltpu.VMEM((2, 32, 256), F32),
            pltpu.VMEM((2, 32, 256), F32),
            pltpu.VMEM((2, 32, 256), F32),
            pltpu.VMEM((4, 4, 2, 32, 128), BF16),
            pltpu.VMEM((4, 4, 32, 128), BF16),
            pltpu.VMEM((2, 4, 4, 16, 128), BF16),
            pltpu.VMEM((4, 16, 128), BF16),
            pltpu.VMEM((4, 16, 128), BF16),
            pltpu.VMEM((4, 16, 128), BF16),
            pltpu.VMEM((6, 32, 128), BF16),
            pltpu.VMEM((6, 32, 128), BF16),
            pltpu.VMEM((6, 32, 128), BF16),
            pltpu.VMEM((4, 32, 128), BF16),
            pltpu.VMEM((4, 32, 128), BF16),
            pltpu.VMEM((4, 64, 128), F32),
            pltpu.VMEM((4, 64, 128), F32),
            pltpu.VMEM((2, 32, 128), F32),
            pltpu.VMEM((32, 128), F32),
            pltpu.SemaphoreType.DMA((11,)),
            pltpu.SemaphoreType.DMA((104,)),
            pltpu.SemaphoreType.DMA((10,)),
            pltpu.SemaphoreType.DMA((10,)),
            pltpu.SemaphoreType.DMA((23,)),
            pltpu.SemaphoreType.DMA((14,)),
            pltpu.SemaphoreType.REGULAR,
            pltpu.SemaphoreType.REGULAR,
        ],
        compiler_params=pltpu.CompilerParams(
            collective_id=0, has_side_effects=True, vmem_limit_bytes=62 * 1024 * 1024
        ),
    )(
        vectors, near_row.reshape(1, 32), near_col.reshape(1, 32), far_row.reshape(1, 128), far_col.reshape(1, 128),
        self_blocks, near_blocks, bases.transpose(0, 2, 1), transfers, couplings.transpose(1, 2, 0),
        root_couplings[0].transpose(1, 2, 0),
    )
    return result.transpose(1, 0, 2)


def solution(mesh):
    both = ("sub", "lvl")
    in_specs = (
        P(both, None, None), P(both, None, None), P(both, None, None), P(both), P(both), P(both, None, None),
        P(both, None, None), P(both), P(both), P(both, None, None), P(both, None, None, None),
    )
    return jax.shard_map(shards, mesh=mesh, in_specs=in_specs, out_specs=P(both, None, None), check_vma=False)
```

```python
import jax
import jax.numpy as jnp
from jax import lax
from jax.experimental import pallas as pl
from jax.experimental.pallas import tpu as pltpu
from jax.sharding import PartitionSpec as P

F32 = jnp.float32
BF16 = jnp.bfloat16
MESH = pl.DeviceIdType.MESH
OFFSETS = (-3, -2, -1, 1, 2, 3)
LEVELS = ((0, 32), (32, 16), (48, 8), (56, 4), (60, 2))


def dot(a, b, ca, cb):
    return lax.dot_general(a, b, (((ca,), (cb,)), ((), ())), preferred_element_type=F32)


def nn(a, b):
    return dot(a, b, 1, 0)


def nt(a, b):
    return dot(a, b, 1, 1)


def tn(a, b):
    return dot(a, b, 0, 0)


def split(x):
    hi = x.astype(BF16)
    return hi, (x - hi.astype(F32)).astype(BF16)


def pick(one_hot, x):
    hi, lo = split(x)
    return nn(one_hot, hi) + nn(one_hot, lo)


def iota(shape, dim):
    return lax.broadcasted_iota(jnp.int32, shape, dim)


def doubled(flat):
    turned = pltpu.roll(flat, 64, 1)
    low = iota(flat.shape, 1) < 64
    return jnp.where(low, flat, turned), jnp.where(low, turned, flat)


def spread(rows, blocks):
    row = iota((16, 128), 0) % 8
    half = iota((16, 128), 1) // 64
    return jnp.concatenate(
        [jnp.where(row == 2 * t + half, rows, 0.0) for t in range(blocks // 2)], axis=1
    )


def collect(wide, blocks):
    row = iota((16, 128), 0) % 8
    half = iota((16, 128), 1) // 64
    total = jnp.zeros((16, 128), F32)
    for t in range(blocks // 2):
        total = total + jnp.where(row == 2 * t + half, wide[:, 128 * t : 128 * t + 128], 0.0)
    return total + pltpu.roll(total, 64, 1)


def joined(rows):
    return jnp.concatenate([rows[0:8, 0:64], rows[8:16, 0:64]], axis=1)


def abreast(rows):
    return jnp.where(iota((8, 128), 1) < 64, rows[0:8], rows[8:16])


def contract(mats, terms, dst):
    t = terms[...]

    def body(i, carry):
        for j in range(8):
            m = mats[8 * i + j]
            for v in range(2):
                row = jnp.sum(m * t[64 * v : 64 * v + 64], axis=0, keepdims=True)
                dst[pl.ds(64 * v + 8 * i + j, 1), :] = row
        return carry

    lax.fori_loop(0, 8, body, 0)


def contract_turned(mats, terms, dst):
    def body(i, carry):
        acc0, acc1 = carry
        for j in range(8):
            m = mats[8 * i + j]
            acc0 = acc0 + m * terms[pl.ds(8 * i + j, 1), :]
            acc1 = acc1 + m * terms[pl.ds(64 + 8 * i + j, 1), :]
        return acc0, acc1

    zero = jnp.zeros((64, 128), F32)
    acc0, acc1 = lax.fori_loop(0, 8, body, (zero, zero))
    dst[0:64, :] = acc0
    dst[64:128, :] = acc1


def tree_up(cs, ps, trans):
    for offset, width in LEVELS:
        count = min(width, 8)
        for g in range(width // count):
            d0, d1 = doubled(cs[8 * g : 8 * g + 8, :])
            lh, ll = split(spread(jnp.concatenate([d0, d1], axis=0), count))
            e = trans[offset + 8 * g : offset + 8 * g + count].reshape(64 * count, 64)
            eh, el = split(e)
            ps[8 * g : 8 * g + 8, :] = joined(nn(lh, eh) + nn(ll, eh) + nn(lh, el))
        half = width // 2
        cs[0:half, :] = ps[pl.ds(0, half, stride=2), :] + ps[pl.ds(1, half, stride=2), :]


def tree_down(fs, halved):
    for offset, width in reversed(LEVELS):
        count = min(width, 8)
        groups = []
        for g in range(width // count):
            f = jnp.concatenate([fs[0, 8 * g : 8 * g + 8, :], fs[1, 8 * g : 8 * g + 8, :]], axis=0)
            fh, fl = split(f[:, 0:64])
            here = slice(offset + 8 * g, offset + 8 * g + count)
            eh = halved[0, here].reshape(64 * count, 64)
            el = halved[1, here].reshape(64 * count, 64)
            main = nt(jnp.concatenate([fh, fl], axis=0), eh)
            groups.append(collect(main[0:16] + main[16:32] + nt(fh, el), count))
        for g, child in enumerate(groups):
            for v in range(2):
                if offset == 0:
                    fs[v, 8 * g : 8 * g + 8, :] = child[8 * v : 8 * v + 8]
                else:
                    fs[v, pl.ds(16 * g, 8, stride=2), :] = child[8 * v : 8 * v + 8]
                    fs[v, pl.ds(16 * g + 1, 8, stride=2), :] = child[8 * v : 8 * v + 8]


def kernel(
    vec_h, near_row_h, near_col_h, far_row_h, far_col_h,
    self_h, near_h, base_h, trans_h, coup_h, root_h,
    out,
    vec, near_row, near_col, far_row, far_col,
    selfs, nears, bases, trans, coup, roots,
    halved, x32, xs, xn, cs, ps, fs, terms, sums, nearp, nwork, back, backin,
    ga, gb, gc, gcin, gq, gqin, nsend, nrecv, cnear, picked, partners, outgoing, incoming, halves, other,
    load_sem, send_sem, a_recv, b_recv, c_recv, o_recv, seen, known,
):
    s = lax.axis_index("sub")
    y = lax.axis_index("lvl")
    z = lax.div(s, 8)
    x = lax.rem(lax.div(s, 2), 4)
    c = lax.rem(s, 2)
    me = s * 4 + y

    def at(x=0, y=0, z=0):
        ox, oy, oz = x, y, z
        return (
            (lax.rem(place["z"] + oz, 4) * 4 + lax.rem(place["x"] + ox, 4)) * 2 + c,
            lax.rem(place["y"] + oy, 4),
        )

    place = {"x": x, "y": y, "z": z}
    sibling = ((z * 4 + x) * 2 + 1 - c, y)

    def shifted(o):
        m = lax.rem(me + o + 128, 128)
        return lax.div(m, 4), lax.rem(m, 4)

    barrier = pltpu.get_barrier_semaphore()
    peers = [at(**{d: o}) for d in "xyz" for o in (1, 2, 3)] + [sibling]
    for peer in peers:
        pl.semaphore_signal(barrier, inc=1, device_id=peer, device_id_type=MESH)

    loads = []
    for i, (src, dst) in enumerate(
        (
            (vec_h, vec), (far_row_h, far_row), (far_col_h, far_col), (near_row_h, near_row), (near_col_h, near_col),
            (base_h, bases), (coup_h, coup), (trans_h, trans), (self_h, selfs), (near_h, nears), (root_h, roots),
        )
    ):
        load = pltpu.make_async_copy(src, dst, load_sem.at[i])
        load.start()
        loads.append(load)

    pending = []

    def send(src, dst, rsem, peer):
        copy = pltpu.make_async_remote_copy(
            src_ref=src, dst_ref=dst, send_sem=send_sem.at[len(pending)], recv_sem=rsem,
            device_id=peer, device_id_type=MESH,
        )
        copy.start()
        pending.append(copy)

    def arrive(dst, rsem):
        pltpu.make_async_remote_copy(
            src_ref=dst, dst_ref=dst, send_sem=send_sem.at[0], recv_sem=rsem,
            device_id=sibling, device_id_type=MESH,
        ).wait_recv()

    def back_by(index, o):
        return lax.rem(index + 4 - o, 4)

    for i in range(5):
        loads[i].wait()
    for v in range(2):
        xv = vec[:, v, :].astype(F32)
        x32[v, 0:32, :] = xv
        xs[v] = xv.astype(BF16)

    row16 = iota((16, 256), 0) % 8
    far_r = far_row[...]
    far_c = far_col[...]
    own_hot = (iota((32, 128), 0) == far_r).astype(BF16)

    def group_rows(ref, g):
        return jnp.concatenate([ref[0, pl.ds(8 * g, 8), :], ref[1, pl.ds(8 * g, 8), :]], axis=0)

    loads[5].wait()

    def coeff_group(g, carry):
        wide = nt(group_rows(x32, g).astype(BF16), bases[pl.ds(8 * g, 8)].reshape(512, 256))
        cs[pl.ds(8 * g, 8), :] = abreast(collect(wide, 8))
        return carry

    lax.fori_loop(0, 4, coeff_group, 0, unroll=True)
    ch, cl = split(cs[...])
    ga[z, x, c] = ch

    terms[...] = tn(ch, own_hot) + tn(cl, own_hot)
    loads[6].wait()
    contract_turned(coup, terms, sums)
    bh, bl = split(sums[...])
    dev = far_c // 32
    dist = (dev - me + 128) % 128
    is_far = (dist > 3) & (dist < 125)
    before = (iota((128, 128), 0) < iota((128, 128), 1)).astype(BF16)
    pos = nn(jnp.broadcast_to(is_far.astype(F32), (16, 128)).astype(BF16), before)[0:1, :].astype(jnp.int32)
    pos = jnp.where(is_far, pos, -1000)
    far_hot = (iota((32, 128), 0) == pos).astype(BF16)
    gb[x, y] = nt(far_hot, bh).astype(BF16)
    lane_hot = (iota((128, 128), 0) == pos + 32 * y).astype(BF16)
    row_id = iota((16, 128), 0)
    codes = jnp.where(row_id == 0, dev, jnp.where(row_id == 1, far_c - dev * 32, 0)).astype(F32).astype(BF16)
    gqin[y] = nt(codes, lane_hot).astype(BF16)
    pl.semaphore_wait(barrier, len(peers))
    send(ga.at[z, x, c], ga.at[z, x, c], a_recv.at[0], sibling)
    for o in (1, 2, 3):
        pl.semaphore_signal(seen, inc=1, device_id=at(x=o), device_id_type=MESH)
        pl.semaphore_signal(seen, inc=1, device_id=at(y=o), device_id_type=MESH)
    for o in (2, 1, 3):
        send(gqin.at[y], gqin.at[y], c_recv.at[16 + o], at(y=o))
        send(gb.at[x, y], gb.at[x, y], b_recv.at[o], at(y=o))

    arrive(ga.at[z, x, 1 - c], a_recv.at[0])
    for o in (2, 1, 3):
        send(ga.at[z, x], ga.at[z, x], a_recv.at[o], at(x=o))
    for o in (2, 1, 3):
        send(ga.at[z, x], ga.at[z, x], a_recv.at[3 + o], at(z=o))
        send(gb.at[x, y], gb.at[x, y], b_recv.at[3 + o], at(x=o))

    leaf_of = iota((32, 128), 0)
    near_hot = jnp.concatenate(
        [(leaf_of + ((me + o + 128) % 128) * 32 == far_c).astype(BF16) for o in OFFSETS], axis=0
    )
    nsend[...] = (nt(near_hot, bh) + nt(near_hot, bl)).astype(BF16).reshape(6, 32, 128)

    loads[7].wait()
    tree_up(cs, ps, trans)
    rh, rl = split(cs[0:1, :])
    tile = jnp.where(row_id == 4 + 2 * y, rh.astype(F32), jnp.where(row_id == 5 + 2 * y, rl.astype(F32), 0.0))
    gcin[y] = tile.astype(BF16)
    for o in (2, 1, 3):
        send(gcin.at[y], gcin.at[y], c_recv.at[o], at(y=o))

    pl.semaphore_wait(seen, 6)
    beside = [at(x=1), at(x=3), at(x=1, z=1), at(x=3, z=3)]
    for peer in beside:
        pl.semaphore_signal(known, inc=1, device_id=peer, device_id_type=MESH)

    def run_blocks(src, dst, blocks, product):
        def body(g, carry):
            rows = group_rows(src, g)
            acc = jnp.zeros((16, 256), F32)
            for j in range(8):
                acc = acc + product(jnp.where(row16 == j, rows, 0.0).astype(BF16), blocks[8 * g + j])
            for v in range(2):
                dst[v, pl.ds(8 * g, 8), :] = acc[8 * v : 8 * v + 8]
            return carry

        lax.fori_loop(0, 4, body, 0, unroll=True)

    loads[8].wait()
    run_blocks(x32, nearp, selfs, nt)

    for o in (1, 3, 2):
        block = ga.at[z, back_by(x, o)]
        arrive(block, a_recv.at[o])
        for p in (2, 1, 3):
            send(block, block, a_recv.at[3 + p], at(z=p))
    for o in (1, 3, 2):
        block = gb.at[x, back_by(y, o)]
        arrive(gqin.at[back_by(y, o)], c_recv.at[16 + o])
        arrive(block, b_recv.at[o])
        for p in (2, 1, 3):
            send(block, block, b_recv.at[3 + p], at(x=p))
    merged = gqin[0].astype(F32) + gqin[1].astype(F32) + gqin[2].astype(F32) + gqin[3].astype(F32)
    gq[x] = merged.astype(BF16)
    for o in (2, 1, 3):
        send(gq.at[x], gq.at[x], c_recv.at[19 + o], at(x=o))

    for o in (1, 3, 2):
        arrive(gcin.at[back_by(y, o)], c_recv.at[o])
    gc[c, z, x] = (
        gcin[0].astype(F32) + gcin[1].astype(F32) + gcin[2].astype(F32) + gcin[3].astype(F32)
    ).astype(BF16)
    for i, j in ((2, 2), (2, 1), (2, 3), (1, 2), (3, 2), (1, 1), (1, 3), (3, 1), (3, 3), (0, 2), (2, 0), (0, 1), (0, 3), (1, 0), (3, 0)):
        k = 4 + 4 * i + (j if i == 0 else 0)
        send(gc.at[c, z, x], gc.at[c, z, x], c_recv.at[k], at(z=i, x=j))

    pl.semaphore_wait(known, len(beside))
    send(xs, xn, o_recv.at[0], shifted(-1))
    for i, o in enumerate(OFFSETS):
        send(ga.at[z, x, c], cnear.at[5 - i], o_recv.at[13 - i], shifted(o))
    for i, o in enumerate(OFFSETS):
        send(nsend.at[i], nrecv.at[i], o_recv.at[2 + i], shifted(o))

    row_hot = (iota((32, 32), 0) == near_row[...]).astype(BF16)
    col_hot = (iota((64, 32), 0) == near_col[...]).astype(BF16)
    for v in range(2):
        nwork[v] = tn(row_hot, xs[v])
    loads[9].wait()
    run_blocks(nwork, nwork, nears, nn)

    for v in range(2):
        both = pick(col_hot, nwork[v])
        nearp[v] = nearp[v] + both[0:32]
        back[v] = both[32:64]

    send(back, backin, o_recv.at[1], shifted(1))

    def decode(t):
        d = t[0:1, :].astype(jnp.int32)
        return d % 4, d // 32, (d // 8) % 4, (d // 4) % 2, t[1:2, :].astype(jnp.int32)

    ty, tz, tx, tc, tleaf = decode(merged)
    slot = jnp.where(ty == y, ((tz * 4 + tx) * 2 + tc) * 32 + tleaf, -1).astype(F32)
    slots = jnp.transpose(jnp.broadcast_to(slot, (128, 128)))
    slot_hot = jnp.concatenate(
        [(slots == (iota((128, 128), 1) + 128 * i).astype(F32)).astype(BF16) for i in range(8)], axis=1
    )

    for j in (1, 3, 2):
        arrive(gq.at[back_by(x, j)], c_recv.at[19 + j])
        arrive(gb.at[back_by(x, j)], b_recv.at[3 + j])
    hots = []
    for j in range(4):
        ty, tz, tx, tc, tleaf = decode(gq[j].astype(F32))
        line = jnp.where((ty == y) & (tx == x), (tz * 2 + tc) * 32 + tleaf, -1)
        hots.append((iota((256, 128), 0) == line).astype(F32).astype(BF16))
    outgoing[...] = nn(jnp.concatenate(hots, axis=1), gb[...].reshape(512, 128)).reshape(4, 64, 128)
    for o in (2, 1, 3):
        to = lax.rem(z + o, 4)
        send(outgoing.at[to], incoming.at[z], b_recv.at[6 + o], at(z=o))
    incoming[z] = outgoing[z]

    for o in (1, 3, 2):
        arrive(ga.at[back_by(z, o)], a_recv.at[3 + o])
    picked[...] = nn(slot_hot, ga[...].reshape(1024, 128)).astype(BF16).reshape(4, 32, 128)
    for o in (2, 1, 3):
        to = lax.rem(y + o, 4)
        send(picked.at[to], partners.at[y], a_recv.at[6 + o], at(y=o))
    partners[y] = picked[y]

    def halve(i, carry):
        hi, lo = split(trans[pl.ds(2 * i, 2)])
        halved[0, pl.ds(2 * i, 2)] = hi
        halved[1, pl.ds(2 * i, 2)] = lo
        return carry

    lax.fori_loop(0, 31, halve, 0)
    row_at = iota((128, 512), 1)
    tile_at = row_at // 16
    line = row_at % 16
    holder = (((tile_at // 4) % 4 * 4 + tile_at % 4) * 2 + tile_at // 16) * 4 + (line - 4) // 2
    sel = ((holder == iota((128, 512), 0)) & (line >= 4) & (line < 12)).astype(BF16)
    for j in (1, 3, 2):
        arrive(gc.at[c, z, back_by(x, j)], c_recv.at[4 + j])
    for i in (1, 3, 2):
        arrive(gc.at[c, back_by(z, i)], c_recv.at[4 + 4 * i])
    send(gc.at[c], gc.at[c], c_recv.at[0], sibling)

    arrive(xn, o_recv.at[0])
    for v in range(2):
        nwork[v] = tn(col_hot, jnp.concatenate([xs[v], xn[v]], axis=0))
    run_blocks(nwork, nwork, nears, nt)
    for v in range(2):
        nearp[v] = nearp[v] + pick(row_hot, nwork[v])

    for o in (1, 3, 2):
        arrive(incoming.at[back_by(z, o)], b_recv.at[6 + o])
    total = incoming[0] + incoming[1] + incoming[2] + incoming[3]
    halves[0] = total[0:32]
    halves[1] = total[32:64]
    send(halves.at[1 - c], other, b_recv.at[0], sibling)
    for i in range(6):
        arrive(cnear.at[i], o_recv.at[8 + i])
    near_terms = tn(cnear[...].reshape(192, 128), near_hot)
    acc = halves[c]
    for i in range(6):
        arrive(nrecv.at[i], o_recv.at[2 + i])
        acc = acc + nrecv[i].astype(F32)

    arrive(gc.at[1 - c], c_recv.at[0])
    terms[...] = jnp.transpose(nn(sel, gc[...].reshape(512, 128)))
    loads[10].wait()
    contract(roots, terms, sums)
    sh, sl = split(sums[...])
    ones = jnp.ones((16, 128), BF16)
    top = (nt(ones, sh) + nt(ones, sl))[0:8]
    d0, d1 = doubled(top)
    fs[0, 0:8, :] = d0
    fs[1, 0:8, :] = d1
    tree_down(fs, halved)

    for o in (1, 3, 2):
        arrive(partners.at[back_by(y, o)], a_recv.at[6 + o])
    rows = partners[0].astype(F32) + partners[1].astype(F32) + partners[2].astype(F32) + partners[3].astype(F32)
    terms[...] = near_terms + tn(rows.astype(BF16), far_hot)
    contract(coup, terms, sums)
    sh, sl = split(sums[...])
    acc = acc + nt(own_hot, sh) + nt(own_hot, sl)
    arrive(other, b_recv.at[0])
    acc = acc + other[...]

    field = acc + jnp.where(iota((32, 128), 1) < 64, fs[0], fs[1])
    d0, d1 = doubled(field.astype(BF16).astype(F32))
    fs[0] = d0
    fs[1] = d1
    arrive(backin, o_recv.at[1])

    def out_group(g, carry):
        lhs = spread(group_rows(fs, g), 8).astype(BF16)
        acc = nn(lhs, bases[pl.ds(8 * g, 8)].reshape(512, 256))
        for v in range(2):
            here = pl.ds(8 * g, 8)
            out[v, here, :] = acc[8 * v : 8 * v + 8] + nearp[v, here, :] + backin[v, here, :]
        return carry

    lax.fori_loop(0, 4, out_group, 0, unroll=True)
    for copy in pending:
        copy.wait_send()


def shards(
    vectors, self_blocks, near_blocks, near_row, near_col, bases, transfers, far_row, far_col, couplings,
    root_couplings,
):
    vmem = pl.BlockSpec(memory_space=pltpu.VMEM)
    hbm = pl.BlockSpec(memory_space=pl.ANY)
    result = pl.pallas_call(
        kernel,
        out_shape=jax.ShapeDtypeStruct((2, 32, 256), F32),
        in_specs=[hbm] * 11,
        out_specs=vmem,
        scratch_shapes=[
            pltpu.VMEM((32, 2, 256), BF16),
            pltpu.VMEM((1, 32), jnp.int32),
            pltpu.VMEM((1, 32), jnp.int32),
            pltpu.VMEM((1, 128), jnp.int32),
            pltpu.VMEM((1, 128), jnp.int32),
            pltpu.VMEM((32, 256, 256), BF16),
            pltpu.VMEM((32, 256, 256), BF16),
            pltpu.VMEM((32, 64, 256), BF16),
            pltpu.VMEM((62, 64, 64), F32),
            pltpu.VMEM((64, 64, 128), F32),
            pltpu.VMEM((64, 64, 128), F32),
            pltpu.VMEM((2, 62, 64, 64), BF16),
            pltpu.VMEM((2, 32, 256), F32),
            pltpu.VMEM((2, 32, 256), BF16),
            pltpu.VMEM((2, 32, 256), BF16),
            pltpu.VMEM((32, 128), F32),
            pltpu.VMEM((32, 128), F32),
            pltpu.VMEM((2, 32, 128), F32),
            pltpu.VMEM((128, 128), F32),
            pltpu.VMEM((128, 128), F32),
            pltpu.VMEM((2, 32, 256), F32),
            pltpu.VMEM((2, 32, 256), F32),
            pltpu.VMEM((2, 32, 256), F32),
            pltpu.VMEM((2, 32, 256), F32),
            pltpu.VMEM((4, 4, 2, 32, 128), BF16),
            pltpu.VMEM((4, 4, 32, 128), BF16),
            pltpu.VMEM((2, 4, 4, 16, 128), BF16),
            pltpu.VMEM((4, 16, 128), BF16),
            pltpu.VMEM((4, 16, 128), BF16),
            pltpu.VMEM((4, 16, 128), BF16),
            pltpu.VMEM((6, 32, 128), BF16),
            pltpu.VMEM((6, 32, 128), BF16),
            pltpu.VMEM((6, 32, 128), BF16),
            pltpu.VMEM((4, 32, 128), BF16),
            pltpu.VMEM((4, 32, 128), BF16),
            pltpu.VMEM((4, 64, 128), F32),
            pltpu.VMEM((4, 64, 128), F32),
            pltpu.VMEM((2, 32, 128), F32),
            pltpu.VMEM((32, 128), F32),
            pltpu.SemaphoreType.DMA((11,)),
            pltpu.SemaphoreType.DMA((104,)),
            pltpu.SemaphoreType.DMA((10,)),
            pltpu.SemaphoreType.DMA((10,)),
            pltpu.SemaphoreType.DMA((23,)),
            pltpu.SemaphoreType.DMA((14,)),
            pltpu.SemaphoreType.REGULAR,
            pltpu.SemaphoreType.REGULAR,
        ],
        compiler_params=pltpu.CompilerParams(
            collective_id=0, has_side_effects=True, vmem_limit_bytes=62 * 1024 * 1024
        ),
    )(
        vectors, near_row.reshape(1, 32), near_col.reshape(1, 32), far_row.reshape(1, 128), far_col.reshape(1, 128),
        self_blocks, near_blocks, bases.transpose(0, 2, 1), transfers, couplings.transpose(1, 2, 0),
        root_couplings[0].transpose(1, 2, 0),
    )
    return result.transpose(1, 0, 2)


def solution(mesh):
    both = ("sub", "lvl")
    in_specs = (
        P(both, None, None), P(both, None, None), P(both, None, None), P(both), P(both), P(both, None, None),
        P(both, None, None), P(both), P(both), P(both, None, None), P(both, None, None, None),
    )
    return jax.shard_map(shards, mesh=mesh, in_specs=in_specs, out_specs=P(both, None, None), check_vma=False)
```
